128 devices in a mesh: dp: 8 (over y, core), tp: 16 (over z, x).
Axes of the slice: x: 4, y: 4, z: 4, core: 2. Of those that a mesh axis runs over, the one named last changes fastest.
Arguments:
- queries: bfloat16 [2, 1024, 128, 576], P(None, ('dp', 'tp')), may hold values from -11 to 11
- latent_cache: bfloat16 [1024, 512, 576], P(('dp', 'tp')), may hold values from -8 to 8
- lengths: int32 [1024], P(('dp', 'tp')), may hold values from 2 to 512, as said below
- inputs: bfloat16 [2, 1024, 4096], P(None, ('dp', 'tp')), may hold values from -9 to 9
- down_latent: bfloat16 [4096, 576], P('tp'), may hold values from -0.09375 to 0.09375
- value_up: bfloat16 [128, 512, 128], P('tp'), may hold values from -0.25 to 0.25
- output_weight: bfloat16 [16384, 4096], P('tp', 'dp'), may hold values from -0.125 to 0.125
- up_weight: bfloat16 [4096, 10240], P(None, 'tp'), may hold values from -0.09375 to 0.09375
- down_weight: bfloat16 [10240, 4096], P('tp'), may hold values from -0.0625 to 0.0625
Outputs:
- layer_out: bfloat16 [2, 1024, 4096], P(None, ('dp', 'tp'))
The draws below stay inside these ranges and needn't reach their ends.
Inputs may be any that keep to these rules, and one draw needn't show every extreme that they name: Row r attends to cache positions below lengths[r]; some row uses all 512 positions.
All inputs are finite; a program needn't handle non-finite values.
Results may differ from the reference program's by a relative error of at most 0.023.
Values may be sent and summed in bfloat16 or wider, within the bound.
A program may use at most 128 MiB of HBM per device.

```python
import jax
import jax.numpy as jnp
from jax import lax

D = 4096
HEADS = 128
LAT = 512
ROPE = 64
VHEAD = 128
FF_W = 10240
CTX = 512
ROWS_DEV = 8
ROWS = 1024


def draw_latent_cache(key, part):
    key = jax.random.fold_in(key, 11)
    result = jnp.clip(jax.random.normal(key, (ROWS, CTX, LAT + ROPE), jnp.float32), -6.0, 6.0)
    return result.astype(jnp.bfloat16)


def draw_queries(key, part):
    key = jax.random.fold_in(key, 13)
    key_base = jax.random.fold_in(key, 0)
    result = jnp.clip(jax.random.normal(key_base, (2, ROWS, HEADS, LAT + ROPE), jnp.float32), -5.0, 5.0)
    return result.astype(jnp.bfloat16)


def draw_inputs(key, part):
    key = jax.random.fold_in(key, 17)
    key_base = jax.random.fold_in(key, 0)
    result = jnp.clip(0.5 * jax.random.normal(key_base, (2, ROWS, D), jnp.float32), -3.0, 3.0)
    return result.astype(jnp.bfloat16)


def draw_lengths(key, part):
    key = jax.random.fold_in(key, 19)
    key_first, key_second, key_pick, key_full = jax.random.split(key, 4)
    first = jax.random.randint(key_first, (ROWS,), 2, CTX + 1)
    second = jax.random.randint(key_second, (ROWS,), 2, CTX + 1)
    pick = jax.random.randint(key_pick, (ROWS,), 0, 4)
    result = jnp.where(pick == 0, first, jnp.minimum(first, second))
    longest = jax.random.randint(key_full, (), 0, ROWS)
    result = result.at[longest].set(CTX)
    return result.astype(jnp.int32)


def block_levels(rng, extent, cuts, least, largest):
    loudness, own = 1.0, jax.random.fold_in(rng, 6)
    for axis_at, blocks in cuts:
        heights = jnp.exp(jax.random.uniform(jax.random.fold_in(own, axis_at), (blocks,), jnp.float32, least / len(cuts), largest / len(cuts)))
        loudness = loudness * jnp.repeat(heights, extent[axis_at] // blocks).reshape([-1 if axis == axis_at else 1 for axis in range(len(extent))])
    return loudness


def centred(own_key, dims, spread, bound, shards=(), kind=jnp.bfloat16):
    entries = jax.random.normal(own_key, dims, jnp.float32) * spread
    if len(shards) > 0:
        entries = block_levels(own_key, dims, shards, -0.22, 0.18) * entries
    return jnp.clip(entries, min=-bound, max=bound).astype(kind)


def setup_inputs(seed: int = 0) -> dict:
    streams_of = jax.random.split(jax.random.key(seed), 10)
    return {
        "queries": draw_queries(jax.random.fold_in(streams_of[9], 71), 0),
        "latent_cache": draw_latent_cache(jax.random.fold_in(streams_of[9], 71), 0),
        "lengths": draw_lengths(jax.random.fold_in(streams_of[9], 71), 0),
        "inputs": draw_inputs(jax.random.fold_in(streams_of[9], 71), 0),
        "down_latent": centred(streams_of[4], (D, LAT + ROPE), D ** -0.5, 0.09375, ((0, 16),)),
        "value_up": centred(streams_of[5], (HEADS, LAT, VHEAD), LAT ** -0.5, 0.25, ((0, 16),)),
        "output_weight": centred(streams_of[6], (HEADS * VHEAD, D), (HEADS * VHEAD // 8) ** -0.5, 0.125, ((0, 16), (1, 8))),
        "up_weight": centred(streams_of[7], (D, FF_W), D ** -0.5, 0.09375, ((1, 16),)),
        "down_weight": centred(streams_of[8], (FF_W, D), FF_W ** -0.5, 0.0625, ((0, 16),)),
    }


EPSILON = 1e-06
SCORE_SCALE = 192.0 ** (-0.5)
ROPE_BASE = 10000.0

def mean_norm(values):
    return values * lax.rsqrt(lax.optimization_barrier(jnp.mean(values * values, axis=-1, keepdims=True)) + EPSILON)

def rotate_pairs(rope_part, positions):
    half_width = rope_part.shape[-1] // 2
    frequency = ROPE_BASE ** (-jnp.arange(half_width, dtype=jnp.float32) / half_width)
    angles = positions.astype(jnp.float32)[:, None] * frequency[None, :]
    first = rope_part[:, :half_width]
    second = rope_part[:, half_width:]
    cosine = jnp.cos(angles)
    sine = jnp.sin(angles)
    return jnp.concatenate([first * cosine - second * sine, second * cosine + first * sine], axis=-1)

def finish_key(compressed, positions):
    latent_part = mean_norm(compressed[:, :LAT])
    rotated = rotate_pairs(compressed[:, LAT:], positions)
    return jnp.concatenate([latent_part, rotated], axis=-1).astype(jnp.bfloat16)

def attend(queries_now, latent_cache, lengths, new_keys):
    query_wide = queries_now.astype(jnp.float32)
    cache_wide = latent_cache.astype(jnp.float32)
    fresh_wide = new_keys.astype(jnp.float32)
    scores = jnp.einsum('rhc,rlc->rhl', query_wide, cache_wide) * SCORE_SCALE
    valid = (jnp.arange(latent_cache.shape[1], dtype=jnp.int32)[None, :] < lengths[:, None])[:, None, :]
    scores = jnp.where(valid, scores, jnp.float32(-1e+30))
    fresh_scores = jnp.einsum('rhc,rkc->rhk', query_wide, fresh_wide) * SCORE_SCALE
    maximum = jnp.maximum(lax.optimization_barrier(jnp.max(scores, axis=-1)), lax.optimization_barrier(jnp.max(fresh_scores, axis=-1)))[..., None]
    weights = jnp.where(valid, jnp.exp(scores - maximum), jnp.float32(0.0))
    fresh_weights = jnp.exp(fresh_scores - maximum)
    denominator = lax.optimization_barrier(jnp.sum(weights, axis=-1, keepdims=True)) + lax.optimization_barrier(jnp.sum(fresh_weights, axis=-1, keepdims=True))
    probability = (weights / denominator).astype(jnp.bfloat16).astype(jnp.float32)
    fresh_probability = (fresh_weights / denominator).astype(jnp.bfloat16).astype(jnp.float32)
    combined = jnp.einsum('rhl,rlc->rhc', probability, cache_wide)
    combined = combined + jnp.einsum('rhk,rkc->rhc', fresh_probability, fresh_wide)
    return combined[..., :LAT].astype(jnp.bfloat16)

def reference(queries, latent_cache, lengths, inputs, down_latent, value_up, output_weight, up_weight, down_weight):
    blocks = ROWS // ROWS_DEV
    width = LAT + ROPE
    new_keys = []
    results = []
    for step in range(2):
        normed = mean_norm(inputs[step].astype(jnp.float32)).astype(jnp.bfloat16)
        compressed = jnp.dot(normed, down_latent, preferred_element_type=jnp.float32)
        new_keys.append(finish_key(compressed, lengths + step))
        stacked = jnp.stack(new_keys, axis=1)

        def one_block(packed):
            return attend(packed[0], packed[1], packed[2], packed[3])
        attended = lax.map(one_block, (queries[step].reshape(blocks, ROWS_DEV, HEADS, width), latent_cache.reshape(blocks, ROWS_DEV, CTX, width), lengths.reshape(blocks, ROWS_DEV), stacked.reshape(blocks, ROWS_DEV, step + 1, width)))
        attended = attended.reshape(ROWS, HEADS, LAT)
        values = jnp.einsum('rhc,hcd->rhd', attended.astype(jnp.float32), value_up.astype(jnp.float32))
        values = values.astype(jnp.bfloat16).reshape(ROWS, HEADS * VHEAD)
        hidden_state = inputs[step].astype(jnp.float32) + jnp.dot(values, output_weight, preferred_element_type=jnp.float32)
        ffn_input = mean_norm(hidden_state).astype(jnp.bfloat16)
        activation = jax.nn.silu(jnp.dot(ffn_input, up_weight, preferred_element_type=jnp.float32)).astype(jnp.bfloat16)
        layer_step = hidden_state + jnp.dot(activation, down_weight, preferred_element_type=jnp.float32)
        results.append(layer_step.astype(jnp.bfloat16))
    return jnp.stack(results, axis=0)
```

```python
import jax
import jax.numpy as jnp
from jax import lax
from jax.experimental import pallas as pl
from jax.experimental.pallas import tpu as pltpu
from jax.sharding import PartitionSpec as P

LAT = 512
WIDTH = 576
CTX = 512
D = 4096
FF = 640
EPSILON = 1e-06
SCORE_SCALE = 192.0 ** (-0.5)
ROPE_BASE = 10000.0
NEG = -1e30
BF = jnp.bfloat16
F32 = jnp.float32
MESH = pl.DeviceIdType.MESH

PLANE = (
    (0, 1), (0, 3), (1, 0), (3, 0), (2, 1), (1, 2), (2, 3), (3, 2),
    (2, 2), (1, 1), (3, 3), (1, 3), (3, 1), (0, 2), (2, 0),
)
LINE = (1, 3, 2)


def copy_to(src, dst, send_sem, recv_sem, device):
    return pltpu.make_async_remote_copy(
        src_ref=src, dst_ref=dst, send_sem=send_sem, recv_sem=recv_sem,
        device_id=device, device_id_type=MESH,
    )


def kernel(
    lens, x_in, cos_in, sin_in, q_hbm, c_hbm, dl_hbm, vu_hbm, ow_hbm, up_hbm, dn_hbm,
    out,
    q_v, c_v, dl_v, vu_v, w_v, up_v, dn_v,
    xs, xr, ps, pr, keys_b, keys_f, o_v, m_v, l_v,
    send_a, recv_a, val_f, val_b,
    c_send1, c_recv1, c_send2, c_recv2, hid, gath, acc, act,
    e_send1, e_recv1, e_send2, e_recv2,
    sem_q, sem_c, sem_w, sem_vu,
    ss_x, rs_x, ss_p, rs_p, ss_a, rs_a, ss_w, rs_w,
    ss_c1, rs_c1, ss_c2, rs_c2, ss_g, rs_g, ss_e1, rs_e1, ss_e2, rs_e2,
):
    dp = lax.axis_index("dp")
    tp = lax.axis_index("tp")
    y, core = dp // 2, dp % 2
    z, x = tp // 4, tp % 4
    plane = [((z + dz) % 4) * 4 + (x + dx) % 4 for dz, dx in PLANE]
    on_x = [z * 4 + (x + k) % 4 for k in LINE]
    on_z = [((z + k) % 4) * 4 + x for k in LINE]
    y_up, y_dn, y_far = (y + 1) % 4, (y + 3) % 4, (y + 2) % 4
    sibling = y * 2 + 1 - core

    def q_copy(r):
        return pltpu.make_async_copy(q_hbm.at[:, r], q_v.at[:, r], sem_q.at[r])

    def c_copy(r):
        return pltpu.make_async_copy(c_hbm.at[r], c_v.at[r], sem_c.at[r])

    dl_copy = pltpu.make_async_copy(dl_hbm, dl_v, sem_w.at[0])
    ow_copy = pltpu.make_async_copy(ow_hbm, w_v.at[dp], sem_w.at[1])
    up_copy = pltpu.make_async_copy(up_hbm, up_v, sem_w.at[2])
    dn_copy = pltpu.make_async_copy(dn_hbm, dn_v, sem_w.at[3])
    vu_copies = [
        pltpu.make_async_copy(vu_hbm.at[h], vu_v.at[:, pl.ds(h * 128, 128)], sem_vu.at[h])
        for h in range(8)
    ]
    for r in range(8):
        q_copy(r).start()
        c_copy(r).start()
        if r == 1:
            dl_copy.start()

    barrier = pltpu.get_barrier_semaphore()
    partners = [(dp, t) for t in plane] + [
        (sibling, tp), (y_up * 2 + core, tp), (y_dn * 2 + core, tp)
    ]
    for device in partners:
        pl.semaphore_signal(barrier, inc=1, device_id=device, device_id_type=MESH)

    x0 = jnp.concatenate([x_in[0].astype(F32), x_in[1].astype(F32)], axis=0)
    scale = lax.rsqrt(jnp.mean(x0 * x0, axis=-1, keepdims=True) + EPSILON)
    xn = (x0 * scale).astype(BF)
    for t in range(16):
        xs[t] = xn[:, t * 256:(t + 1) * 256]
    xr[tp] = xs[tp]

    pl.semaphore_wait(barrier, len(partners))

    x_copies = [
        copy_to(xs.at[t], xr.at[tp], ss_x.at[k], rs_x.at[k], (dp, t))
        for k, t in enumerate(plane)
    ]
    for c in x_copies:
        c.start()

    lo, hi = pl.ds(0, 512), pl.ds(512, 512)
    up_dev, dn_dev, sib_dev = (y_up * 2 + core, tp), (y_dn * 2 + core, tp), (sibling, tp)
    w_up = [
        copy_to(ow_hbm.at[s], w_v.at[dp, s], ss_w.at[i], rs_w.at[i], up_dev)
        for i, s in enumerate((lo, hi))
    ]
    w_dn = [
        copy_to(ow_hbm.at[s], w_v.at[dp, s], ss_w.at[2 + i], rs_w.at[2 + i], dn_dev)
        for i, s in enumerate((hi, lo))
    ]
    w_sib = copy_to(ow_hbm, w_v.at[dp], ss_w.at[4], rs_w.at[4], sib_dev)
    from_dn, from_up, from_far = y_dn * 2 + core, y_up * 2 + core, y_far * 2 + core
    w_up2 = copy_to(w_v.at[from_dn, lo], w_v.at[from_dn, lo], ss_w.at[5], rs_w.at[5], up_dev)
    w_dn2 = copy_to(w_v.at[from_up, hi], w_v.at[from_up, hi], ss_w.at[6], rs_w.at[6], dn_dev)
    w_sib_dn = copy_to(w_v.at[from_dn], w_v.at[from_dn], ss_w.at[7], rs_w.at[7], sib_dev)
    w_sib_up = copy_to(w_v.at[from_up], w_v.at[from_up], ss_w.at[8], rs_w.at[8], sib_dev)
    w_sib_far = copy_to(w_v.at[from_far], w_v.at[from_far], ss_w.at[9], rs_w.at[9], sib_dev)
    for c in (w_up[0], w_dn[0], w_up[1], w_dn[1], w_sib):
        c.start()
    ow_copy.start()

    def attend_row(r, carry):
        q_copy(r).wait()
        c_copy(r).wait()
        q = jnp.concatenate([q_v[0, r], q_v[1, r]], axis=0)
        k = c_v[r]
        s = lax.dot_general(
            q, k, (((1,), (1,)), ((), ())), preferred_element_type=F32
        ) * SCORE_SCALE
        position = lax.broadcasted_iota(jnp.int32, (1, CTX), 1)
        s = jnp.where(position < lens[r], s, NEG)
        m = jnp.max(s, axis=-1, keepdims=True)
        p = jnp.exp(s - m)
        l_v[r] = jnp.sum(p, axis=-1, keepdims=True)
        m_v[r] = m
        o_v[r] = jnp.dot(p.astype(BF), k[:, :LAT], preferred_element_type=F32)
        return carry

    lax.fori_loop(0, 4, attend_row, 0)

    for c in vu_copies:
        c.start()
    up_copy.start()
    dn_copy.start()

    dl_copy.wait()
    for c in x_copies:
        c.wait_recv()
    partial = jnp.dot(xr[...].reshape(256, 256), dl_v[...], preferred_element_type=F32)
    ps[...] = partial.astype(BF).reshape(16, 16, WIDTH)
    p_copies = [
        copy_to(ps.at[t], pr.at[k], ss_p.at[k], rs_p.at[k], (dp, t))
        for k, t in enumerate(plane)
    ]
    for c in p_copies:
        c.start()

    lax.fori_loop(4, 8, attend_row, 0)

    for c in p_copies:
        c.wait_recv()
    comp = ps[tp].astype(F32)
    for k in range(15):
        comp = comp + pr[k].astype(F32)
    lat = comp[:, :LAT]
    lat = lat * lax.rsqrt(jnp.mean(lat * lat, axis=-1, keepdims=True) + EPSILON)
    rope = comp[:, LAT:]
    swapped = jnp.concatenate([rope[:, 32:], rope[:, :32]], axis=-1)
    rotated = rope * cos_in[...] + swapped * sin_in[...]
    keys_b[:, :LAT] = lat.astype(BF)
    keys_b[:, LAT:] = rotated.astype(BF)
    keys_f[...] = lat.astype(BF).astype(F32)

    def a_copies(i):
        rows = pl.ds(2 * i, 2)
        return [
            copy_to(send_a.at[rows, t], recv_a.at[rows, tp], ss_a.at[i, k], rs_a.at[i, k], (dp, t))
            for k, t in enumerate(plane)
        ]

    def finish_row(r):
        q = jnp.concatenate([q_v[0, r], q_v[1, r]], axis=0)
        fresh = lax.dot_general(
            q, keys_b[...], (((1,), (1,)), ((), ())), preferred_element_type=F32
        ) * SCORE_SCALE
        lane = lax.broadcasted_iota(jnp.int32, (256, 16), 1)
        row = lax.broadcasted_iota(jnp.int32, (256, 1), 0)
        s0 = jnp.sum(jnp.where(lane == r, fresh, 0.0), axis=-1, keepdims=True)
        s1 = jnp.sum(jnp.where(lane == r + 8, fresh, 0.0), axis=-1, keepdims=True)
        s1 = jnp.where(row >= 128, s1, NEG)
        m_old = m_v[r]
        m = jnp.maximum(jnp.maximum(m_old, s0), s1)
        keep = jnp.exp(m_old - m)
        p0 = jnp.exp(s0 - m)
        p1 = jnp.exp(s1 - m)
        inverse = 1.0 / (keep * l_v[r] + p0 + p1)
        k0 = keys_f[pl.ds(r, 1), :]
        k1 = keys_f[pl.ds(r + 8, 1), :]
        o = o_v[r] * (keep * inverse) + (p0 * inverse) * k0 + (p1 * inverse) * k1
        pieces = []
        for t in range(16):
            pieces += [o[t * 8:t * 8 + 8], o[128 + t * 8:128 + t * 8 + 8]]
        send_a[r] = jnp.concatenate(pieces, axis=0).astype(BF).reshape(16, 16, LAT)
        recv_a[r, tp] = send_a[r, tp]

    def finish_pair(i, carry):
        finish_row(2 * i)
        finish_row(2 * i + 1)
        for c in a_copies(i):
            c.start()
        return carry

    lax.fori_loop(0, 4, finish_pair, 0)

    w_up[0].wait_recv()
    w_up2.start()
    w_dn[0].wait_recv()
    w_dn2.start()
    w_up[1].wait_recv()
    w_sib_dn.start()
    w_dn[1].wait_recv()
    w_sib_up.start()

    for c in vu_copies:
        c.wait()

    def values_pair(i, carry):
        for c in a_copies(i):
            c.wait_recv()
        head = lax.broadcasted_iota(jnp.int32, (8, 128), 0)[None]
        for j in range(2):
            a = recv_a[2 * i + j].reshape(256, LAT)
            full = jnp.dot(a, vu_v[...], preferred_element_type=F32)
            full = full.reshape(32, 8, 1024)
            own = jnp.where(head == 0, full[:, :, :128], 0.0)
            for h in range(1, 8):
                own = jnp.where(head == h, full[:, :, h * 128:(h + 1) * 128], own)
            for b in range(32):
                at = pl.multiple_of(b * 64 + (2 * i + j) * 8, 8)
                val_f[pl.ds(at, 8), :] = own[b]
        return carry

    lax.fori_loop(0, 4, values_pair, 0)
    for h in range(8):
        val_b[:, h * 128:(h + 1) * 128] = val_f[pl.ds(h, 256, stride=8), :].astype(BF)

    w_up2.wait_recv()
    w_dn2.wait_recv()
    w_sib_far.start()
    ow_copy.wait()

    def stage1(i, send1, recv1, ss, rs):
        first = [
            copy_to(send1.at[i, 0, :, (x + k) % 4], recv1.at[i, 0, n],
                    ss.at[i, 0, n], rs.at[i, 0, n], (dp, on_x[n]))
            for n, k in enumerate(LINE)
        ]
        second = [
            copy_to(send1.at[i, 1, (z + k) % 4], recv1.at[i, 1, n],
                    ss.at[i, 1, n], rs.at[i, 1, n], (dp, on_z[n]))
            for n, k in enumerate(LINE)
        ]
        return first + second

    def stage2(i, send2, recv2, ss, rs):
        first = [
            copy_to(send2.at[i, 0, (z + k) % 4], recv2.at[i, 0, n],
                    ss.at[i, 0, n], rs.at[i, 0, n], (dp, on_z[n]))
            for n, k in enumerate(LINE)
        ]
        second = [
            copy_to(send2.at[i, 1, (x + k) % 4], recv2.at[i, 1, n],
                    ss.at[i, 1, n], rs.at[i, 1, n], (dp, on_x[n]))
            for n, k in enumerate(LINE)
        ]
        return first + second

    def group_sum(multiply, before, send1, recv1, send2, recv2, ss1, rs1, ss2, rs2):
        def middle(i):
            for c in stage1(i, send1, recv1, ss1, rs1):
                c.wait_recv()
            for way, own in ((0, send1[i, 0, :, x]), (1, send1[i, 1, z])):
                total = own.astype(F32)
                for n in range(3):
                    total = total + recv1[i, way, n].astype(F32)
                send2[i, way] = total.astype(BF)
            for c in stage2(i, send2, recv2, ss2, rs2):
                c.start()

        def step(i, carry):
            before(i)
            for way in range(2):
                send1[i, way] = multiply(i, way).astype(BF).reshape(4, 4, 16, 512)
            for c in stage1(i, send1, recv1, ss1, rs1):
                c.start()

            @pl.when(i > 0)
            def _():
                middle(i - 1)

            return carry

        lax.fori_loop(0, 4, step, 0)
        middle(3)

    def summed(i, way, send2, recv2):
        total = send2[i, way, z if way == 0 else x].astype(F32)
        for n in range(3):
            total = total + recv2[i, way, n].astype(F32)
        return total

    def block_of(i):
        return (y + i + i // 2 - 2 * (i // 3)) % 4

    def before_c(i):
        @pl.when(i == 0)
        def _():
            w_sib.wait_recv()

        @pl.when(i == 1)
        def _():
            w_sib_up.wait_recv()

        @pl.when(i == 2)
        def _():
            w_sib_dn.wait_recv()

        @pl.when(i == 3)
        def _():
            w_sib_far.wait_recv()

    group_sum(
        lambda i, way: jnp.dot(
            val_b[...], w_v[block_of(i) * 2 + way], preferred_element_type=F32
        ),
        before_c, c_send1, c_recv1, c_send2, c_recv2, ss_c1, rs_c1, ss_c2, rs_c2,
    )

    def take_c(i, carry):
        for c in stage2(i, c_send2, c_recv2, ss_c2, rs_c2):
            c.wait_recv()
        for way in range(2):
            hid[block_of(i) * 2 + way] = summed(i, way, c_send2, c_recv2)
        return carry

    lax.fori_loop(0, 4, take_c, 0)

    square = jnp.zeros((16, 1), F32)
    for j in range(8):
        cols = slice(j * 512, (j + 1) * 512)
        part = jnp.concatenate([x_in[0, :, cols].astype(F32), x_in[1, :, cols].astype(F32)], axis=0)
        part = part + hid[j]
        hid[j] = part
        square = square + jnp.sum(part * part, axis=-1, keepdims=True)
    scale = lax.rsqrt(square / D + EPSILON)
    for j in range(8):
        gath[j // 4, z, x, :, (j % 4) * 512:(j % 4 + 1) * 512] = (hid[j] * scale).astype(BF)

    def g_copy(way, at_z, at_x, device, n):
        block = gath.at[way, at_z, at_x]
        return copy_to(block, block, ss_g.at[way, n], rs_g.at[way, n], (dp, device))

    g_first = [
        [g_copy(0, z, x, on_x[n], n) for n in range(3)],
        [g_copy(1, z, x, on_z[n], n) for n in range(3)],
    ]
    g_own = [
        [g_copy(0, z, x, on_z[n], 3 + n) for n in range(3)],
        [g_copy(1, z, x, on_x[n], 3 + n) for n in range(3)],
    ]
    for n in range(3):
        for way in range(2):
            g_first[way][n].start()
    for n in range(3):
        for way in range(2):
            g_own[way][n].start()
    g_pass = [[], []]
    for m, k in enumerate(LINE):
        g_first[0][m].wait_recv()
        for n in range(3):
            c = g_copy(0, z, (x + 4 - k) % 4, on_z[n], 6 + 3 * m + n)
            c.start()
            g_pass[0].append(c)
        g_first[1][m].wait_recv()
        for n in range(3):
            c = g_copy(1, (z + 4 - k) % 4, x, on_x[n], 6 + 3 * m + n)
            c.start()
            g_pass[1].append(c)

    up_copy.wait()
    acc[...] = jnp.zeros_like(acc)
    for way in range(2):
        for c in g_own[way] + g_pass[way]:
            c.wait_recv()
        for j in range(4):
            a = gath[way, :, :, :, j * 512:(j + 1) * 512].reshape(256, 512)
            at = way * 2048 + j * 512
            acc[...] += jnp.dot(a, up_v[at:at + 512, :], preferred_element_type=F32)
    v = acc[...]
    act[...] = (v / (1.0 + jnp.exp(-v))).astype(BF)

    dn_copy.wait()
    group_sum(
        lambda i, way: jnp.dot(
            act[...], dn_v[:, pl.ds(pl.multiple_of(i * 1024 + way * 512, 512), 512)],
            preferred_element_type=F32,
        ),
        lambda i: None, e_send1, e_recv1, e_send2, e_recv2, ss_e1, rs_e1, ss_e2, rs_e2,
    )
    for i in range(4):
        for c in stage2(i, e_send2, e_recv2, ss_e2, rs_e2):
            c.wait_recv()
        for way in range(2):
            total = hid[2 * i + way] + summed(i, way, e_send2, e_recv2)
            cols = slice(i * 1024 + way * 512, i * 1024 + (way + 1) * 512)
            out[0, :, cols] = total[:8].astype(BF)
            out[1, :, cols] = total[8:].astype(BF)

    for c in x_copies + p_copies:
        c.wait_send()

    def drain(i, carry):
        for c in a_copies(i):
            c.wait_send()
        for c in stage1(i, c_send1, c_recv1, ss_c1, rs_c1) + stage2(i, c_send2, c_recv2, ss_c2, rs_c2):
            c.wait_send()
        for c in stage1(i, e_send1, e_recv1, ss_e1, rs_e1) + stage2(i, e_send2, e_recv2, ss_e2, rs_e2):
            c.wait_send()
        return carry

    lax.fori_loop(0, 4, drain, 0)
    for c in w_up + w_dn + [w_sib, w_up2, w_dn2, w_sib_dn, w_sib_up, w_sib_far]:
        c.wait_send()
    for way in range(2):
        for c in g_first[way] + g_own[way] + g_pass[way]:
            c.wait_send()


def layer(lengths, inputs, cosine, sine, queries, cache, down_latent, value_up, output_weight, up_weight, down_weight):
    vmem, hbm = pl.BlockSpec(memory_space=pltpu.VMEM), pl.BlockSpec(memory_space=pl.ANY)
    dma = pltpu.SemaphoreType.DMA
    scratch = [
        pltpu.VMEM((2, 8, 128, WIDTH), BF),
        pltpu.VMEM((8, CTX, WIDTH), BF),
        pltpu.VMEM((256, WIDTH), BF),
        pltpu.VMEM((LAT, 1024), BF),
        pltpu.VMEM((8, 1024, 512), BF),
        pltpu.VMEM((D, FF), BF),
        pltpu.VMEM((FF, D), BF),
        pltpu.VMEM((16, 16, 256), BF),
        pltpu.VMEM((16, 16, 256), BF),
        pltpu.VMEM((16, 16, WIDTH), BF),
        pltpu.VMEM((15, 16, WIDTH), BF),
        pltpu.VMEM((16, WIDTH), BF),
        pltpu.VMEM((16, LAT), F32),
        pltpu.VMEM((8, 256, LAT), F32),
        pltpu.VMEM((8, 256, 1), F32),
        pltpu.VMEM((8, 256, 1), F32),
        pltpu.VMEM((8, 16, 16, LAT), BF),
        pltpu.VMEM((8, 16, 16, LAT), BF),
        pltpu.VMEM((2048, 128), F32),
        pltpu.VMEM((256, 1024), BF),
    ]
    sums = [
        pltpu.VMEM((4, 2, 4, 4, 16, 512), BF),
        pltpu.VMEM((4, 2, 3, 4, 16, 512), BF),
        pltpu.VMEM((4, 2, 4, 16, 512), BF),
        pltpu.VMEM((4, 2, 3, 16, 512), BF),
    ]
    scratch += sums + [
        pltpu.VMEM((8, 16, 512), F32),
        pltpu.VMEM((2, 4, 4, 16, 2048), BF),
        pltpu.VMEM((256, FF), F32),
        pltpu.VMEM((256, FF), BF),
    ] + sums
    scratch += [dma((8,)), dma((8,)), dma((4,)), dma((8,))]
    scratch += [dma((15,))] * 4 + [dma((4, 15))] * 2 + [dma((10,))] * 2
    scratch += [dma((4, 2, 3))] * 4 + [dma((2, 15))] * 2 + [dma((4, 2, 3))] * 4
    return pl.pallas_call(
        kernel,
        out_shape=jax.ShapeDtypeStruct((2, 8, D), BF),
        in_specs=[pl.BlockSpec(memory_space=pltpu.SMEM)] + [vmem] * 3 + [hbm] * 7,
        out_specs=vmem,
        scratch_shapes=scratch,
        compiler_params=pltpu.CompilerParams(
            collective_id=0, has_side_effects=True, vmem_limit_bytes=60 * 1024 * 1024
        ),
    )(lengths, inputs, cosine, sine, queries, cache, down_latent, value_up, output_weight, up_weight, down_weight)


def body(queries, latent_cache, lengths, inputs, down_latent, value_up, output_weight, up_weight, down_weight):
    frequency = ROPE_BASE ** (-jnp.arange(32, dtype=F32) / 32)
    position = jnp.concatenate([lengths, lengths + 1]).astype(F32)
    angles = position[:, None] * frequency[None, :]
    cosine, sine = jnp.cos(angles), jnp.sin(angles)
    return layer(
        lengths, inputs,
        jnp.concatenate([cosine, cosine], axis=-1), jnp.concatenate([-sine, sine], axis=-1),
        queries, latent_cache, down_latent, value_up, output_weight, up_weight, down_weight,
    )


def solution(mesh):
    return jax.shard_map(
        body,
        mesh=mesh,
        in_specs=(
            P(None, ("dp", "tp"), None, None),
            P(("dp", "tp"), None, None),
            P(("dp", "tp")),
            P(None, ("dp", "tp"), None),
            P("tp", None),
            P("tp", None, None),
            P("tp", "dp"),
            P(None, "tp"),
            P("tp", None),
        ),
        out_specs=P(None, ("dp", "tp"), None),
        check_vma=False,
    )
```

```python
import math

import jax
import jax.numpy as jnp
import numpy as np
from jax import lax
from jax.experimental import pallas as pl
from jax.experimental.pallas import tpu as pltpu
from jax.sharding import PartitionSpec as P

LAT = 512
WIDTH = 576
CTX = 512
D = 4096
FF = 640
EPSILON = 1e-06
SCORE_SCALE = 192.0 ** (-0.5)
ROPE_BASE = 10000.0
NEG = -1e30
BF = jnp.bfloat16
F32 = jnp.float32
MESH = pl.DeviceIdType.MESH

PLANE = (
    (0, 1), (0, 3), (1, 0), (3, 0), (2, 1), (1, 2), (2, 3), (3, 2),
    (2, 2), (1, 1), (3, 3), (1, 3), (3, 1), (0, 2), (2, 0),
)
LINE = (1, 3, 2)


def copy_to(src, dst, send_sem, recv_sem, device):
    return pltpu.make_async_remote_copy(
        src_ref=src, dst_ref=dst, send_sem=send_sem, recv_sem=recv_sem,
        device_id=device, device_id_type=MESH,
    )


def cos_sin(angles):
    turns = jnp.floor(angles * (0.5 / np.pi) + 0.5)
    rest = angles - turns * 6.28125
    rest = rest - turns * (2 * np.pi - 6.28125)
    square = rest * rest
    cosine = jnp.zeros_like(square)
    sine = jnp.zeros_like(square)
    for n in range(8, -1, -1):
        cosine = cosine * square + (-1.0) ** n / math.factorial(2 * n)
        sine = sine * square + (-1.0) ** n / math.factorial(2 * n + 1)
    return cosine, sine * rest


def kernel(
    lens, x_hbm, freq_hbm, q_hbm, c_hbm, dl_hbm, vu_hbm, ow_hbm, up_hbm, dn_hbm,
    out,
    x_in, freq_in, q_v, c_v, dl_v, vu_v, w_v, up_v, dn_v,
    xr, ps, pr, keys_b, keys_f, o_v, m_v, l_v,
    send_a, recv_a, val_f, val_b, hid, acc, square, act,
    mix_s, mix_r, key_s, key_r, keep_f, fresh_f,
    c_send1, c_recv1, c_send2, c_recv2, gath, c_tail1, c_tail2, c_tail3, c_tail4, gath_tail,
    e_send1, e_recv1, e_send2, e_recv2, e_tail1, e_tail2, e_tail3, e_tail4,
    sem_q, sem_c, sem_w, sem_vu,
    ss_x, rs_x, ss_p, rs_p, ss_a, rs_a, ss_m, rs_m, ss_k, rs_k, ss_w, rs_w, ss_g, rs_g,
    ss_c1, rs_c1, ss_c2, rs_c2, ss_e1, rs_e1, ss_e2, rs_e2,
):
    dp = lax.axis_index("dp")
    tp = lax.axis_index("tp")
    y, core = dp // 2, dp % 2
    z, x = tp // 4, tp % 4
    plane = [((z + dz) % 4) * 4 + (x + dx) % 4 for dz, dx in PLANE]
    on_x = {k: (dp, z * 4 + (x + k) % 4) for k in LINE}
    on_z = {k: (dp, ((z + k) % 4) * 4 + x) for k in LINE}
    y_up, y_dn, y_far = (y + 1) % 4, (y + 3) % 4, (y + 2) % 4
    sibling = y * 2 + 1 - core

    barrier = pltpu.get_barrier_semaphore()
    partners = [(dp, t) for t in plane] + [
        (sibling, tp), (y_up * 2 + core, tp), (y_dn * 2 + core, tp)
    ]
    for device in partners:
        pl.semaphore_signal(barrier, inc=1, device_id=device, device_id_type=MESH)

    def q_copy(r):
        return pltpu.make_async_copy(q_hbm.at[:, r], q_v.at[:, r], sem_q.at[r])

    def c_copy(r):
        return pltpu.make_async_copy(c_hbm.at[r], c_v.at[r], sem_c.at[r])

    dl_copy = pltpu.make_async_copy(dl_hbm, dl_v, sem_w.at[0])
    ow_copy = pltpu.make_async_copy(ow_hbm, w_v.at[dp], sem_w.at[1])
    up_copy = pltpu.make_async_copy(up_hbm, up_v, sem_w.at[2])
    dn_copy = pltpu.make_async_copy(dn_hbm, dn_v, sem_w.at[3])
    x_copy = pltpu.make_async_copy(x_hbm, x_in, sem_w.at[4])
    freq_copy = pltpu.make_async_copy(freq_hbm, freq_in, sem_w.at[5])
    vu_copies = [
        pltpu.make_async_copy(vu_hbm.at[h], vu_v.at[:, pl.ds(h * 128, 128)], sem_vu.at[h])
        for h in range(8)
    ]
    x_copy.start()
    for r in range(8):
        q_copy(r).start()
        c_copy(r).start()
        if r == 1:
            dl_copy.start()
            freq_copy.start()

    pl.semaphore_wait(barrier, len(partners))

    def x_slice(t):
        return x_hbm.at[:, :, pl.ds(pl.multiple_of(t * 256, 256), 256)]

    x_copies = [
        copy_to(x_slice(t), xr.at[tp], ss_x.at[k], rs_x.at[k], (dp, t))
        for k, t in enumerate(plane)
    ]
    for c in x_copies:
        c.start()
    x_own = pltpu.make_async_copy(x_slice(tp), xr.at[tp], sem_w.at[6])
    x_own.start()

    lo, hi = pl.ds(0, 512), pl.ds(512, 512)
    up_dev, dn_dev, sib_dev = (y_up * 2 + core, tp), (y_dn * 2 + core, tp), (sibling, tp)
    w_up = [
        copy_to(ow_hbm.at[s], w_v.at[dp, s], ss_w.at[i], rs_w.at[i], up_dev)
        for i, s in enumerate((lo, hi))
    ]
    w_dn = [
        copy_to(ow_hbm.at[s], w_v.at[dp, s], ss_w.at[2 + i], rs_w.at[2 + i], dn_dev)
        for i, s in enumerate((hi, lo))
    ]
    w_sib = copy_to(ow_hbm, w_v.at[dp], ss_w.at[4], rs_w.at[4], sib_dev)
    from_dn, from_up, from_far = y_dn * 2 + core, y_up * 2 + core, y_far * 2 + core
    w_up2 = copy_to(w_v.at[from_dn, lo], w_v.at[from_dn, lo], ss_w.at[5], rs_w.at[5], up_dev)
    w_dn2 = copy_to(w_v.at[from_up, hi], w_v.at[from_up, hi], ss_w.at[6], rs_w.at[6], dn_dev)
    w_sib_dn = copy_to(w_v.at[from_dn], w_v.at[from_dn], ss_w.at[7], rs_w.at[7], sib_dev)
    w_sib_up = copy_to(w_v.at[from_up], w_v.at[from_up], ss_w.at[8], rs_w.at[8], sib_dev)
    w_sib_far = copy_to(w_v.at[from_far], w_v.at[from_far], ss_w.at[9], rs_w.at[9], sib_dev)
    for c in (w_up[0], w_dn[0], w_up[1], w_dn[1], w_sib):
        c.start()
    ow_copy.start()

    def a_copies(step, g):
        rows = pl.ds(2 * g, 2)
        return [
            copy_to(send_a.at[step, rows, t], recv_a.at[step, rows, tp],
                    ss_a.at[step, g, k], rs_a.at[step, g, k], (dp, t))
            for k, t in enumerate(plane)
        ]

    def attend_row(r):
        q_copy(r).wait()
        c_copy(r).wait()
        q = jnp.concatenate([q_v[0, r], q_v[1, r]], axis=1)
        k = c_v[r]
        s = lax.dot_general(
            q, k, (((0,), (0,)), ((), ())), preferred_element_type=F32
        ) * SCORE_SCALE
        position = lax.broadcasted_iota(jnp.int32, (1, CTX), 1)
        s = jnp.where(position < lens[r], s, NEG)
        m = jnp.max(s, axis=-1, keepdims=True)
        p = jnp.exp(s - m)
        total = jnp.sum(p, axis=-1, keepdims=True)
        l_v[r] = total
        m_v[r] = m
        o = lax.dot_general(
            p.astype(BF), k[:LAT], (((1,), (1,)), ((), ())), preferred_element_type=F32
        )
        o_v[r] = o[128:]
        return (o[:128] * (1.0 / total[:128])).reshape(16, 8, LAT)

    def attend_pair(pair, carry):
        both = [attend_row(2 * pair), attend_row(2 * pair + 1)]
        send_a[0, pair] = jnp.concatenate(both, axis=1).astype(BF)
        recv_a[0, pair, tp] = send_a[0, pair, tp]
        return carry

    lax.fori_loop(0, 1, attend_pair, 0)

    for c in vu_copies:
        c.start()
    up_copy.start()
    dn_copy.start()

    dl_copy.wait()
    x_own.wait()
    for c in x_copies:
        c.wait_recv()
    partial = lax.dot_general(
        xr[...].astype(F32).reshape(256, 256).astype(BF), dl_v[...], (((1,), (1,)), ((), ())),
        preferred_element_type=F32,
    )
    ps[...] = partial.astype(BF).reshape(16, 16, WIDTH)
    p_copies = [
        copy_to(ps.at[t], pr.at[k], ss_p.at[k], rs_p.at[k], (dp, t))
        for k, t in enumerate(plane)
    ]
    for c in p_copies:
        c.start()

    def attend_and_send(pair, carry):
        attend_pair(pair, carry)

        @pl.when(pair % 2 == 1)
        def _():
            for c in a_copies(0, pair // 2):
                c.start()

        return carry

    lax.fori_loop(1, 4, attend_and_send, 0)

    freq_copy.wait()
    x_copy.wait()
    x0 = jnp.concatenate([x_in[0].astype(F32), x_in[1].astype(F32)], axis=0)
    x_scale = lax.rsqrt(jnp.mean(x0 * x0, axis=-1, keepdims=True) + EPSILON)
    for c in p_copies:
        c.wait_recv()
    comp = ps[tp].astype(F32)
    for k in range(15):
        comp = comp + pr[k].astype(F32)
    comp = comp * x_scale
    lat = comp[:, :LAT]
    lat = lat * lax.rsqrt(jnp.mean(lat * lat, axis=-1, keepdims=True) + EPSILON)
    rope = comp[:, LAT:]
    swapped = jnp.concatenate([rope[:, 32:], rope[:, :32]], axis=-1)
    row = lax.broadcasted_iota(jnp.int32, (16, 64), 0)
    position = row // 8
    for r in range(8):
        position = position + jnp.where(row % 8 == r, lens[r], 0)
    cosine, sine = cos_sin(position.astype(F32) * freq_in[...])
    first = lax.broadcasted_iota(jnp.int32, (16, 64), 1) < 32
    rotated = rope * cosine + swapped * jnp.where(first, -sine, sine)
    keys_b[:, :LAT] = lat.astype(BF)
    keys_b[:, LAT:] = rotated.astype(BF)
    keys_f[...] = lat.astype(BF).astype(F32)

    key_s[...] = jnp.concatenate([lat[:8, :256], lat[:8, 256:]], axis=0).astype(BF)
    key_r[tp] = key_s[...]
    k_copies = [
        copy_to(key_s, key_r.at[tp], ss_k.at[k], rs_k.at[k], (dp, t)) for k, t in enumerate(plane)
    ]
    for c in k_copies:
        c.start()

    def fresh_scores(step, r):
        fresh = jnp.dot(keys_b[...], q_v[step, r], preferred_element_type=F32).T * SCORE_SCALE
        lane = lax.broadcasted_iota(jnp.int32, (128, 16), 1)
        s0 = jnp.sum(jnp.where(lane == r, fresh, 0.0), axis=-1, keepdims=True)
        s1 = jnp.sum(jnp.where(lane == r + 8, fresh, 0.0), axis=-1, keepdims=True)
        return s0, s1

    def mix_row(r, mix):
        s0, _ = fresh_scores(0, r)
        m_old = m_v[r, :128]
        m = jnp.maximum(m_old, s0)
        cached = jnp.exp(m_old - m) * l_v[r, :128]
        p0 = jnp.exp(s0 - m)
        inverse = 1.0 / (cached + p0)
        lane = lax.broadcasted_iota(jnp.int32, (128, 128), 1)
        mix = jnp.where(lane == r, cached * inverse, mix)
        return jnp.where(lane == r + 8, p0 * inverse, mix)

    mix = lax.fori_loop(0, 8, mix_row, jnp.zeros((128, 128), F32))
    mix_s[...] = mix.reshape(16, 8, 128)
    mix_r[tp] = mix_s[tp]
    m_copies = [
        copy_to(mix_s.at[t], mix_r.at[tp], ss_m.at[k], rs_m.at[k], (dp, t))
        for k, t in enumerate(plane)
    ]
    for c in m_copies:
        c.start()

    def finish_row(r):
        s0, s1 = fresh_scores(1, r)
        m_old = m_v[r, 128:]
        m = jnp.maximum(jnp.maximum(m_old, s0), s1)
        keep = jnp.exp(m_old - m)
        p0 = jnp.exp(s0 - m)
        p1 = jnp.exp(s1 - m)
        inverse = 1.0 / (keep * l_v[r, 128:] + p0 + p1)
        k0 = keys_f[pl.ds(r, 1), :]
        k1 = keys_f[pl.ds(r + 8, 1), :]
        o = o_v[r] * (keep * inverse) + (p0 * inverse) * k0 + (p1 * inverse) * k1
        return o.reshape(16, 8, LAT)

    def finish_four(g, carry):
        for j in range(2):
            pair = 2 * g + j
            both = [finish_row(2 * pair), finish_row(2 * pair + 1)]
            send_a[1, pair] = jnp.concatenate(both, axis=1).astype(BF)
            recv_a[1, pair, tp] = send_a[1, pair, tp]
        for c in a_copies(1, g):
            c.start()
        return carry

    lax.fori_loop(0, 2, finish_four, 0)

    def values(step):
        def four(g, carry):
            for c in a_copies(step, g):
                c.wait_recv()
            head = lax.broadcasted_iota(jnp.int32, (8, 128), 0)[None]
            for j in range(2):
                pair = 2 * g + j
                a = recv_a[step, pair].reshape(256, LAT)
                full = jnp.dot(a, vu_v[...], preferred_element_type=F32)
                full = full.reshape(32, 8, 1024)
                own = jnp.where(head == 0, full[:, :, :128], 0.0)
                for h in range(1, 8):
                    own = jnp.where(head == h, full[:, :, h * 128:(h + 1) * 128], own)
                for b in range(32):
                    at = pl.multiple_of((b // 2) * 64 + (2 * pair + b % 2) * 8, 8)
                    val_f[pl.ds(at, 8), :] = own[b]
            return carry

        lax.fori_loop(0, 2, four, 0)
        if step == 0:
            for c in k_copies + m_copies:
                c.wait_recv()

            def spread(src, carry):
                tile = mix_r[src]
                for r in range(8):
                    at = pl.ds(pl.multiple_of(src * 64 + r * 8, 8), 8)
                    keep_f[at, :] = jnp.broadcast_to(tile[:, r:r + 1], (8, 128))
                    fresh_f[at, :] = jnp.broadcast_to(tile[:, r + 8:r + 9], (8, 128))
                return carry

            lax.fori_loop(0, 16, spread, 0)
            keys = key_r[...].astype(F32)
            keys = jnp.concatenate([keys[:, :8], keys[:, 8:]], axis=2).reshape(128, LAT).astype(BF)
            projected = jnp.dot(keys, vu_v[...], preferred_element_type=F32)
        for h in range(8):
            cols = slice(h * 128, (h + 1) * 128)
            own = pl.ds(h, 128, stride=8)
            if step == 0:
                mixed = keep_f[own, :] * val_f[own, :] + fresh_f[own, :] * projected[:, cols]
                val_b[0, :, cols] = mixed.astype(BF)
            else:
                val_b[1, :, cols] = val_f[own, :].astype(BF)

    def ways(order):
        return ((order[0:3], order[3:6]), (order[6:7], order[7:8]))

    c_cols = ways([b * 2 + c for b in (y, y_up, y_dn, y_far) for c in range(2)])
    e_cols = ways(list(range(8)))

    def fold(a):
        return jnp.concatenate([a[..., :256], a[..., 256:]], axis=-2)

    def unfold(a):
        return jnp.concatenate([a[..., :8, :], a[..., 8:, :]], axis=-1)

    class Sum:
        def __init__(self, cols, parts, sems):
            self.cols, self.parts = cols, parts
            self.ss1, self.rs1, self.ss2, self.rs2 = sems

        def share(self, step, i, way, k):
            send1 = self.parts[i][0]
            if way == 0:
                return send1.at[step, 0, :, (x + k) % 4]
            return send1.at[step, 1, (z + k) % 4]

        def first(self, step, i, way, n):
            on = on_x if way == 0 else on_z
            k = LINE[n]
            return copy_to(self.share(step, i, way, k), self.parts[i][1].at[step, way, n],
                           self.ss1.at[step, i, way, n], self.rs1.at[step, i, way, n], on[k])

        def last(self, step, i, way, n):
            on, here = (on_z, z) if way == 0 else (on_x, x)
            k = LINE[n]
            return copy_to(self.parts[i][2].at[step, way, (here + k) % 4], self.parts[i][3].at[step, way, n],
                           self.ss2.at[step, i, way, n], self.rs2.at[step, i, way, n], on[k])

        def begin(self, step, i, multiply):
            for way in range(2):
                for m, col in enumerate(self.cols[i][way]):
                    block = fold(multiply(col).reshape(16, 8, 512)).astype(BF)
                    self.parts[i][0][step, way, :, :, :, m * 256:(m + 1) * 256] = block.reshape(4, 4, 16, 256)
                for n in range(3):
                    self.first(step, i, way, n).start()

        def middle(self, step, i):
            for way in range(2):
                total = self.share(step, i, way, 0)[...].astype(F32)
                for n in range(3):
                    self.first(step, i, way, n).wait_recv()
                    total = total + self.parts[i][1][step, way, n].astype(F32)
                self.parts[i][2][step, way] = total.astype(BF)
                for n in range(3):
                    self.last(step, i, way, n).start()

        def end(self, step, i, way):
            total = self.parts[i][2][step, way, z if way == 0 else x].astype(F32)
            for n in range(3):
                self.last(step, i, way, n).wait_recv()
                total = total + self.parts[i][3][step, way, n].astype(F32)
            return total

        def drain(self):
            for step in range(2):
                for i in range(2):
                    for way in range(2):
                        for n in range(3):
                            self.first(step, i, way, n).wait_send()
                            self.last(step, i, way, n).wait_send()

    c_sum = Sum(
        c_cols,
        ((c_send1, c_recv1, c_send2, c_recv2), (c_tail1, c_tail2, c_tail3, c_tail4)),
        (ss_c1, rs_c1, ss_c2, rs_c2),
    )
    e_sum = Sum(
        e_cols,
        ((e_send1, e_recv1, e_send2, e_recv2), (e_tail1, e_tail2, e_tail3, e_tail4)),
        (ss_e1, rs_e1, ss_e2, rs_e2),
    )

    def begin_c(step, i):
        c_sum.begin(step, i, lambda col: jnp.dot(
            val_b[step], w_v[col], preferred_element_type=F32
        ))

    rows_in = (gath, gath_tail)

    def g_first(step, i, way, n):
        on = on_x if way == 0 else on_z
        block = rows_in[i].at[step, way, z, x]
        return copy_to(block, block, ss_g.at[step, i, way, n], rs_g.at[step, i, way, n], on[LINE[n]])

    def g_last(step, i, way, n):
        on = on_z if way == 0 else on_x
        block = rows_in[i].at[step, 0, z] if way == 0 else rows_in[i].at[step, 1, :, x]
        return copy_to(block, block, ss_g.at[step, i, way, 3 + n], rs_g.at[step, i, way, 3 + n], on[LINE[n]])

    def hidden(step, i):
        for way in range(2):
            total = c_sum.end(step, i, way)
            for m, col in enumerate(c_cols[i][way]):
                own = x_in[step, :, pl.ds(pl.multiple_of(col * 512, 512), 512)].astype(F32)
                here = slice(m * 256, (m + 1) * 256)
                block = total[:, here] + fold(own)
                hid[step, col] = block
                rows_in[i][step, way, z, x, :, here] = block.astype(BF)
            for n in range(3):
                g_first(step, i, way, n).start()

    def gather(step, i):
        for way in range(2):
            for n in range(3):
                g_first(step, i, way, n).wait_recv()
            for n in range(3):
                g_last(step, i, way, n).start()

    def expand(step, i):
        total = None
        squares = None
        for way in range(2):
            for n in range(3):
                g_last(step, i, way, n).wait_recv()
            for m, col in enumerate(c_cols[i][way]):
                rows = rows_in[i][step, way, :, :, :, m * 256:(m + 1) * 256].reshape(16, 16, 256)
                a = unfold(rows.astype(F32)).reshape(128, 512)
                more = jnp.sum(a * a, axis=-1, keepdims=True)
                term = jnp.dot(a.astype(BF), up_v[col], preferred_element_type=F32)
                total = term if total is None else total + term
                squares = more if squares is None else squares + more
        if i == 0:
            acc[step] = total
            square[step] = squares
        else:
            v = (acc[step] + total) * lax.rsqrt((square[step] + squares) / D + EPSILON)
            act[step] = (v / (1.0 + jnp.exp(-v))).astype(BF)

    def begin_e(step, i):
        e_sum.begin(step, i, lambda col: jnp.dot(
            act[step], dn_v[:, col * 512:(col + 1) * 512], preferred_element_type=F32
        ))

    def finish(step, i):
        for way in range(2):
            total = e_sum.end(step, i, way)
            for m, col in enumerate(e_cols[i][way]):
                result = unfold(hid[step, col] + total[:, m * 256:(m + 1) * 256])
                out[step, :, col * 512:(col + 1) * 512] = result.astype(BF)

    def weights_near():
        w_up[1].wait_recv()
        w_dn[1].wait_recv()
        w_sib_up.start()
        w_sib_dn.start()
        ow_copy.wait()
        w_sib.wait_recv()
        w_sib_up.wait_recv()
        w_sib_dn.wait_recv()

    def weights_far():
        w_up2.wait_recv()
        w_dn2.wait_recv()
        w_sib_far.start()
        w_sib_far.wait_recv()

    w_up[0].wait_recv()
    w_up2.start()
    w_dn[0].wait_recv()
    w_dn2.start()
    for c in vu_copies:
        c.wait()
    values(0)
    weights_near()
    begin_c(0, 0)
    values(1)
    begin_c(1, 0)
    c_sum.middle(0, 0)
    weights_far()
    begin_c(0, 1)
    begin_c(1, 1)
    c_sum.middle(1, 0)
    hidden(0, 0)
    c_sum.middle(0, 1)
    c_sum.middle(1, 1)
    hidden(1, 0)
    hidden(0, 1)
    gather(0, 0)
    gather(0, 1)
    hidden(1, 1)
    gather(1, 0)
    up_copy.wait()
    expand(0, 0)
    gather(1, 1)
    expand(0, 1)
    dn_copy.wait()
    begin_e(0, 0)
    expand(1, 0)
    begin_e(0, 1)
    expand(1, 1)
    begin_e(1, 0)
    begin_e(1, 1)
    e_sum.middle(0, 0)
    e_sum.middle(0, 1)
    e_sum.middle(1, 0)
    e_sum.middle(1, 1)
    finish(0, 0)
    finish(0, 1)
    finish(1, 0)
    finish(1, 1)

    for c in x_copies + p_copies + k_copies + m_copies:
        c.wait_send()

    def drain(i, carry):
        for c in a_copies(i // 2, i % 2):
            c.wait_send()
        return carry

    lax.fori_loop(0, 4, drain, 0)
    for c in w_up + w_dn + [w_sib, w_up2, w_dn2, w_sib_dn, w_sib_up, w_sib_far]:
        c.wait_send()
    c_sum.drain()
    e_sum.drain()
    for step in range(2):
        for i in range(2):
            for way in range(2):
                for n in range(3):
                    g_first(step, i, way, n).wait_send()
                    g_last(step, i, way, n).wait_send()


def layer(lengths, inputs, frequency, queries, cache, down_latent, value_up, output_weight, up_weight, down_weight):
    vmem, hbm = pl.BlockSpec(memory_space=pltpu.VMEM), pl.BlockSpec(memory_space=pl.ANY)
    dma = pltpu.SemaphoreType.DMA
    scratch = [
        pltpu.VMEM((2, 8, D), BF),
        pltpu.VMEM((16, 64), F32),
        pltpu.VMEM((2, 8, WIDTH, 128), BF),
        pltpu.VMEM((8, WIDTH, CTX), BF),
        pltpu.VMEM((WIDTH, 256), BF),
        pltpu.VMEM((LAT, 1024), BF),
        pltpu.VMEM((8, 1024, 512), BF),
        pltpu.VMEM((8, 512, FF), BF),
        pltpu.VMEM((FF, D), BF),
        pltpu.VMEM((16, 2, 8, 256), BF),
        pltpu.VMEM((16, 16, WIDTH), BF),
        pltpu.VMEM((15, 16, WIDTH), BF),
        pltpu.VMEM((16, WIDTH), BF),
        pltpu.VMEM((16, LAT), F32),
        pltpu.VMEM((8, 128, LAT), F32),
        pltpu.VMEM((8, 256, 1), F32),
        pltpu.VMEM((8, 256, 1), F32),
        pltpu.VMEM((2, 4, 16, 16, LAT), BF),
        pltpu.VMEM((2, 4, 16, 16, LAT), BF),
        pltpu.VMEM((1024, 128), F32),
        pltpu.VMEM((2, 128, 1024), BF),
        pltpu.VMEM((2, 8, 16, 256), F32),
        pltpu.VMEM((2, 128, FF), F32),
        pltpu.VMEM((2, 128, 1), F32),
        pltpu.VMEM((2, 128, FF), BF),
    ]
    scratch += [
        pltpu.VMEM((16, 8, 128), F32),
        pltpu.VMEM((16, 8, 128), F32),
        pltpu.VMEM((16, 256), BF),
        pltpu.VMEM((16, 16, 256), BF),
        pltpu.VMEM((1024, 128), F32),
        pltpu.VMEM((1024, 128), F32),
    ]
    for gathers in (1, 0):
        for width in (768, 256):
            scratch += [
                pltpu.VMEM((2, 2, 4, 4, 16, width), BF),
                pltpu.VMEM((2, 2, 3, 4, 16, width), BF),
                pltpu.VMEM((2, 2, 4, 16, width), BF),
                pltpu.VMEM((2, 2, 3, 16, width), BF),
            ] + [pltpu.VMEM((2, 2, 4, 4, 16, width), BF)] * gathers
    scratch += [dma((8,)), dma((8,)), dma((7,)), dma((8,))]
    scratch += [dma((15,))] * 4 + [dma((2, 2, 15))] * 2 + [dma((15,))] * 4 + [dma((10,))] * 2 + [dma((2, 2, 2, 6))] * 2
    scratch += [dma((2, 2, 2, 3))] * 8
    return pl.pallas_call(
        kernel,
        out_shape=jax.ShapeDtypeStruct((2, 8, D), BF),
        in_specs=[pl.BlockSpec(memory_space=pltpu.SMEM)] + [hbm] * 9,
        out_specs=vmem,
        scratch_shapes=scratch,
        compiler_params=pltpu.CompilerParams(
            collective_id=0, has_side_effects=True, vmem_limit_bytes=60 * 1024 * 1024
        ),
    )(lengths, inputs, frequency, queries, cache, down_latent, value_up, output_weight, up_weight, down_weight)


def body(queries, latent_cache, lengths, inputs, down_latent, value_up, output_weight, up_weight, down_weight):
    half = ROPE_BASE ** (-np.arange(32, dtype=np.float32) / np.float32(32))
    frequency = np.tile(half.astype(np.float32), (16, 2))
    return layer(
        lengths, inputs, jnp.asarray(frequency),
        jnp.swapaxes(queries, 2, 3), jnp.swapaxes(latent_cache, 1, 2), down_latent.T,
        value_up, output_weight, up_weight.reshape(8, 512, FF), down_weight,
    )


def solution(mesh):
    return jax.shard_map(
        body,
        mesh=mesh,
        in_specs=(
            P(None, ("dp", "tp"), None, None),
            P(("dp", "tp"), None, None),
            P(("dp", "tp")),
            P(None, ("dp", "tp"), None),
            P("tp", None),
            P("tp", None, None),
            P("tp", "dp"),
            P(None, "tp"),
            P("tp", None),
        ),
        out_specs=P(None, ("dp", "tp"), None),
        check_vma=False,
    )
```

```python
import math

import jax
import jax.numpy as jnp
import numpy as np
from jax import lax
from jax.experimental import pallas as pl
from jax.experimental.pallas import tpu as pltpu
from jax.sharding import PartitionSpec as P

LAT = 512
WIDTH = 576
CTX = 512
D = 4096
FF = 640
EPSILON = 1e-06
SCORE_SCALE = 192.0 ** (-0.5)
ROPE_BASE = 10000.0
NEG = -1e30
BF = jnp.bfloat16
F32 = jnp.float32
MESH = pl.DeviceIdType.MESH

PLANE = (
    (0, 1), (0, 3), (1, 0), (3, 0), (2, 1), (1, 2), (2, 3), (3, 2),
    (2, 2), (1, 1), (3, 3), (1, 3), (3, 1), (0, 2), (2, 0),
)
LINE = (1, 3, 2)


def copy_to(src, dst, send_sem, recv_sem, device):
    return pltpu.make_async_remote_copy(
        src_ref=src, dst_ref=dst, send_sem=send_sem, recv_sem=recv_sem,
        device_id=device, device_id_type=MESH,
    )


def all_of(region, send_sem, recv_sem, device):
    return copy_to(region, region, send_sem, recv_sem, device)


def cos_sin(angles):
    turns = jnp.floor(angles * (0.5 / np.pi) + 0.5)
    rest = angles - turns * 6.28125
    rest = rest - turns * (2 * np.pi - 6.28125)
    square = rest * rest
    cosine = jnp.zeros_like(square)
    sine = jnp.zeros_like(square)
    for n in range(8, -1, -1):
        cosine = cosine * square + (-1.0) ** n / math.factorial(2 * n)
        sine = sine * square + (-1.0) ** n / math.factorial(2 * n + 1)
    return cosine, sine * rest


def kernel(
    lens, x_hbm, freq_hbm, q_hbm, c_hbm, dl_hbm, vu_hbm, ow_hbm, up_hbm, dn_hbm,
    out,
    x_in, freq_in, q_v, c_v, dl_v, vu_v, w_v, up_v, dn_v,
    xr, ps, pr, keys_b, keys_f, o_v, m_v, l_v,
    send_a, recv_a, val_f, val_b, hid, acc, square, act,
    mix_s, mix_r, key_s, key_r, keep_f, fresh_f,
    c_send1, c_recv1, c_send2, c_recv2, gath, c_tail1, c_tail2, c_tail3, c_tail4, gath_tail,
    e_send1, e_recv1, e_send2, e_recv2, e_tail1, e_tail2, e_tail3, e_tail4,
    sem_q, sem_c, sem_w, sem_vu,
    ss_x, rs_x, ss_p, rs_p, ss_a, rs_a, ss_m, rs_m, ss_k, rs_k, ss_w, rs_w, ss_g, rs_g,
    ss_c1, rs_c1, ss_c2, rs_c2, ss_e1, rs_e1, ss_e2, rs_e2,
):
    dp = lax.axis_index("dp")
    tp = lax.axis_index("tp")
    y, core = dp // 2, dp % 2
    z, x = tp // 4, tp % 4
    plane = [((z + dz) % 4) * 4 + (x + dx) % 4 for dz, dx in PLANE]
    on_x = {k: (dp, z * 4 + (x + k) % 4) for k in LINE}
    on_z = {k: (dp, ((z + k) % 4) * 4 + x) for k in LINE}
    next_device = (dp, plane[0])
    y_up, y_dn, y_far = (y + 1) % 4, (y + 3) % 4, (y + 2) % 4
    sibling = y * 2 + 1 - core

    barrier = pltpu.get_barrier_semaphore()
    partners = [(dp, t) for t in plane] + [
        (sibling, tp), (y_up * 2 + core, tp), (y_dn * 2 + core, tp)
    ]
    for device in partners:
        pl.semaphore_signal(barrier, inc=1, device_id=device, device_id_type=MESH)

    def q_copy(r):
        return pltpu.make_async_copy(q_hbm.at[:, r], q_v.at[:, r], sem_q.at[r])

    def c_copy(r):
        return pltpu.make_async_copy(c_hbm.at[r], c_v.at[r], sem_c.at[r])

    dl_copy = pltpu.make_async_copy(dl_hbm, dl_v, sem_w.at[0])
    ow_copy = pltpu.make_async_copy(ow_hbm, w_v.at[dp], sem_w.at[1])
    up_copy = pltpu.make_async_copy(up_hbm, up_v, sem_w.at[2])
    dn_copy = pltpu.make_async_copy(dn_hbm, dn_v, sem_w.at[3])
    x_copy = pltpu.make_async_copy(x_hbm, x_in, sem_w.at[4])
    freq_copy = pltpu.make_async_copy(freq_hbm, freq_in, sem_w.at[5])
    vu_copies = [
        pltpu.make_async_copy(vu_hbm.at[h], vu_v.at[:, pl.ds(h * 128, 128)], sem_vu.at[h])
        for h in range(8)
    ]
    x_copy.start()
    for r in range(2):
        q_copy(r).start()
        c_copy(r).start()
    dl_copy.start()

    pl.semaphore_wait(barrier, len(partners))

    def x_slice(t):
        return x_hbm.at[:, :, pl.ds(pl.multiple_of(t * 256, 256), 256)]

    x_copies = [
        copy_to(x_slice(t), xr.at[tp], ss_x, rs_x, (dp, t))
        for k, t in enumerate(plane)
    ]
    for c in x_copies:
        c.start()
    x_all = all_of(xr.at[pl.ds(0, 15)], ss_x, rs_x, next_device)
    for r in range(2, 8):
        q_copy(r).start()
        c_copy(r).start()
    freq_copy.start()
    x_own = pltpu.make_async_copy(x_slice(tp), xr.at[tp], sem_w.at[6])
    x_own.start()

    lo, hi = pl.ds(0, 512), pl.ds(512, 512)
    up_dev, dn_dev, sib_dev = (y_up * 2 + core, tp), (y_dn * 2 + core, tp), (sibling, tp)
    w_up = [
        copy_to(ow_hbm.at[s], w_v.at[dp, s], ss_w.at[i], rs_w.at[i], up_dev)
        for i, s in enumerate((lo, hi))
    ]
    w_dn = [
        copy_to(ow_hbm.at[s], w_v.at[dp, s], ss_w.at[2 + i], rs_w.at[2 + i], dn_dev)
        for i, s in enumerate((hi, lo))
    ]
    w_sib = copy_to(ow_hbm, w_v.at[dp], ss_w.at[4], rs_w.at[4], sib_dev)
    from_dn, from_up, from_far = y_dn * 2 + core, y_up * 2 + core, y_far * 2 + core
    w_up2 = copy_to(w_v.at[from_dn, lo], w_v.at[from_dn, lo], ss_w.at[5], rs_w.at[5], up_dev)
    w_dn2 = copy_to(w_v.at[from_up, hi], w_v.at[from_up, hi], ss_w.at[6], rs_w.at[6], dn_dev)
    w_sib_dn = copy_to(w_v.at[from_dn], w_v.at[from_dn], ss_w.at[7], rs_w.at[7], sib_dev)
    w_sib_up = copy_to(w_v.at[from_up], w_v.at[from_up], ss_w.at[8], rs_w.at[8], sib_dev)
    w_sib_far = copy_to(w_v.at[from_far], w_v.at[from_far], ss_w.at[9], rs_w.at[9], sib_dev)
    for c in (w_up[0], w_dn[0], w_up[1], w_dn[1], w_sib):
        c.start()
    ow_copy.start()

    def a_copies(step, g):
        rows = pl.ds(2 * g, 2)
        return [
            copy_to(send_a.at[step, rows, t], recv_a.at[step, rows, tp],
                    ss_a.at[step, g], rs_a.at[step, g], (dp, t))
            for t in plane
        ]

    def a_pair(pair):
        return [
            copy_to(send_a.at[0, pair, t], recv_a.at[0, pair, tp],
                    ss_a.at[0, pair // 2], rs_a.at[0, pair // 2], (dp, t))
            for t in plane
        ]

    def a_all(step, g):
        return all_of(recv_a.at[step, pl.ds(2 * g, 2), pl.ds(0, 15)],
                      ss_a.at[step, g], rs_a.at[step, g], next_device)

    def attend_row(r):
        q_copy(r).wait()
        c_copy(r).wait()
        q = jnp.concatenate([q_v[0, r], q_v[1, r]], axis=1)
        k = c_v[r]
        s = lax.dot_general(
            q, k, (((0,), (0,)), ((), ())), preferred_element_type=F32
        ) * SCORE_SCALE
        position = lax.broadcasted_iota(jnp.int32, (1, CTX), 1)
        s = jnp.where(position < lens[r], s, NEG)
        m = jnp.max(s, axis=-1, keepdims=True)
        p = jnp.exp(s - m)
        total = jnp.sum(p, axis=-1, keepdims=True)
        l_v[r] = total
        m_v[r] = m
        o = lax.dot_general(
            p.astype(BF), k[:LAT], (((1,), (1,)), ((), ())), preferred_element_type=F32
        )
        o_v[r] = o[128:]
        return (o[:128] * (1.0 / total[:128])).reshape(16, 8, LAT)

    def attend_pair(pair, carry):
        both = [attend_row(2 * pair), attend_row(2 * pair + 1)]
        send_a[0, pair] = jnp.concatenate(both, axis=1).astype(BF)
        recv_a[0, pair, tp] = send_a[0, pair, tp]
        return carry

    lax.fori_loop(0, 1, attend_pair, 0)

    for c in vu_copies:
        c.start()
    up_copy.start()
    dn_copy.start()

    dl_copy.wait()
    x_own.wait()
    x_all.wait_recv()
    partial = lax.dot_general(
        xr[...].astype(F32).reshape(256, 256).astype(BF), dl_v[...], (((1,), (1,)), ((), ())),
        preferred_element_type=F32,
    )
    ps[...] = partial.astype(BF).reshape(16, 16, WIDTH)
    p_copies = [
        copy_to(ps.at[t], pr.at[k], ss_p, rs_p, (dp, t))
        for k, t in enumerate(plane)
    ]
    for c in p_copies:
        c.start()
    p_all = all_of(pr, ss_p, rs_p, next_device)
    for c in a_pair(0):
        c.start()

    def attend_and_send(pair, carry):
        attend_pair(pair, carry)
        for c in a_pair(pair):
            c.start()
        return carry

    lax.fori_loop(1, 4, attend_and_send, 0)

    freq_copy.wait()
    x_copy.wait()
    x0 = jnp.concatenate([x_in[0].astype(F32), x_in[1].astype(F32)], axis=0)
    x_scale = lax.rsqrt(jnp.mean(x0 * x0, axis=-1, keepdims=True) + EPSILON)
    p_all.wait_recv()
    comp = ps[tp].astype(F32)
    for k in range(15):
        comp = comp + pr[k].astype(F32)
    comp = comp * x_scale
    lat = comp[:, :LAT]
    lat = lat * lax.rsqrt(jnp.mean(lat * lat, axis=-1, keepdims=True) + EPSILON)
    rope = comp[:, LAT:]
    swapped = jnp.concatenate([rope[:, 32:], rope[:, :32]], axis=-1)
    row = lax.broadcasted_iota(jnp.int32, (16, 64), 0)
    position = row // 8
    for r in range(8):
        position = position + jnp.where(row % 8 == r, lens[r], 0)
    cosine, sine = cos_sin(position.astype(F32) * freq_in[...])
    first = lax.broadcasted_iota(jnp.int32, (16, 64), 1) < 32
    rotated = rope * cosine + swapped * jnp.where(first, -sine, sine)
    keys_b[:, :LAT] = lat.astype(BF)
    keys_b[:, LAT:] = rotated.astype(BF)
    keys_f[...] = lat.astype(BF).astype(F32)

    key_s[...] = jnp.concatenate([lat[:8, :256], lat[:8, 256:]], axis=0).astype(BF)
    key_r[tp] = key_s[...]
    k_copies = [
        copy_to(key_s, key_r.at[tp], ss_k, rs_k, (dp, t)) for k, t in enumerate(plane)
    ]
    for c in k_copies:
        c.start()
    k_all = all_of(key_r.at[pl.ds(0, 15)], ss_k, rs_k, next_device)

    def fresh_scores(step, r):
        fresh = jnp.dot(keys_b[...], q_v[step, r], preferred_element_type=F32).T * SCORE_SCALE
        lane = lax.broadcasted_iota(jnp.int32, (128, 16), 1)
        s0 = jnp.sum(jnp.where(lane == r, fresh, 0.0), axis=-1, keepdims=True)
        s1 = jnp.sum(jnp.where(lane == r + 8, fresh, 0.0), axis=-1, keepdims=True)
        return s0, s1

    def mix_row(r, mix):
        s0, _ = fresh_scores(0, r)
        m_old = m_v[r, :128]
        m = jnp.maximum(m_old, s0)
        cached = jnp.exp(m_old - m) * l_v[r, :128]
        p0 = jnp.exp(s0 - m)
        inverse = 1.0 / (cached + p0)
        lane = lax.broadcasted_iota(jnp.int32, (128, 128), 1)
        mix = jnp.where(lane == r, cached * inverse, mix)
        return jnp.where(lane == r + 8, p0 * inverse, mix)

    mix = lax.fori_loop(0, 8, mix_row, jnp.zeros((128, 128), F32))
    mix_s[...] = mix.reshape(16, 8, 128)
    mix_r[tp] = mix_s[tp]
    m_copies = [
        copy_to(mix_s.at[t], mix_r.at[tp], ss_m, rs_m, (dp, t))
        for k, t in enumerate(plane)
    ]
    for c in m_copies:
        c.start()
    m_all = all_of(mix_r.at[pl.ds(0, 15)], ss_m, rs_m, next_device)

    def finish_row(r):
        s0, s1 = fresh_scores(1, r)
        m_old = m_v[r, 128:]
        m = jnp.maximum(jnp.maximum(m_old, s0), s1)
        keep = jnp.exp(m_old - m)
        p0 = jnp.exp(s0 - m)
        p1 = jnp.exp(s1 - m)
        inverse = 1.0 / (keep * l_v[r, 128:] + p0 + p1)
        k0 = keys_f[pl.ds(r, 1), :]
        k1 = keys_f[pl.ds(r + 8, 1), :]
        o = o_v[r] * (keep * inverse) + (p0 * inverse) * k0 + (p1 * inverse) * k1
        return o.reshape(16, 8, LAT)

    def finish_four(g, carry):
        for j in range(2):
            pair = 2 * g + j
            both = [finish_row(2 * pair), finish_row(2 * pair + 1)]
            send_a[1, pair] = jnp.concatenate(both, axis=1).astype(BF)
            recv_a[1, pair, tp] = send_a[1, pair, tp]
        for c in a_copies(1, g):
            c.start()
        return carry

    lax.fori_loop(0, 2, finish_four, 0)

    def values(step):
        def four(g, carry):
            a_all(step, g).wait_recv()
            head = lax.broadcasted_iota(jnp.int32, (8, 128), 0)[None]
            for j in range(2):
                pair = 2 * g + j
                a = recv_a[step, pair].reshape(256, LAT)
                full = jnp.dot(a, vu_v[...], preferred_element_type=F32)
                full = full.reshape(32, 8, 1024)
                own = jnp.where(head == 0, full[:, :, :128], 0.0)
                for h in range(1, 8):
                    own = jnp.where(head == h, full[:, :, h * 128:(h + 1) * 128], own)
                for b in range(32):
                    at = pl.multiple_of((b // 2) * 64 + (2 * pair + b % 2) * 8, 8)
                    val_f[pl.ds(at, 8), :] = own[b]
            return carry

        lax.fori_loop(0, 2, four, 0)
        if step == 0:
            k_all.wait_recv()
            m_all.wait_recv()

            def spread(src, carry):
                tile = mix_r[src]
                for r in range(8):
                    at = pl.ds(pl.multiple_of(src * 64 + r * 8, 8), 8)
                    keep_f[at, :] = jnp.broadcast_to(tile[:, r:r + 1], (8, 128))
                    fresh_f[at, :] = jnp.broadcast_to(tile[:, r + 8:r + 9], (8, 128))
                return carry

            lax.fori_loop(0, 16, spread, 0)
            keys = key_r[...].astype(F32)
            keys = jnp.concatenate([keys[:, :8], keys[:, 8:]], axis=2).reshape(128, LAT).astype(BF)
            projected = jnp.dot(keys, vu_v[...], preferred_element_type=F32)
        for h in range(8):
            cols = slice(h * 128, (h + 1) * 128)
            own = pl.ds(h, 128, stride=8)
            if step == 0:
                mixed = keep_f[own, :] * val_f[own, :] + fresh_f[own, :] * projected[:, cols]
                val_b[0, :, cols] = mixed.astype(BF)
            else:
                val_b[1, :, cols] = val_f[own, :].astype(BF)

    def ways(order):
        return ((order[0:3], order[3:6]), (order[6:7], order[7:8]))

    c_cols = ways([b * 2 + c for b in (y, y_up, y_dn, y_far) for c in range(2)])
    e_cols = ways(list(range(8)))

    def fold(a):
        return jnp.concatenate([a[..., :256], a[..., 256:]], axis=-2)

    def unfold(a):
        return jnp.concatenate([a[..., :8, :], a[..., 8:, :]], axis=-1)

    class Sum:
        def __init__(self, cols, parts, sems):
            self.cols, self.parts = cols, parts
            self.ss1, self.rs1, self.ss2, self.rs2 = sems

        def share(self, step, i, way, k):
            send1 = self.parts[i][0]
            if way == 0:
                return send1.at[step, 0, :, (x + k) % 4]
            return send1.at[step, 1, (z + k) % 4]

        def first(self, step, i, way, n):
            on = on_x if way == 0 else on_z
            k = LINE[n]
            return copy_to(self.share(step, i, way, k), self.parts[i][1].at[step, way, n],
                           self.ss1.at[step, i, way], self.rs1.at[step, i, way], on[k])

        def last(self, step, i, way, n):
            on, here = (on_z, z) if way == 0 else (on_x, x)
            k = LINE[n]
            return copy_to(self.parts[i][2].at[step, way, (here + k) % 4], self.parts[i][3].at[step, way, n],
                           self.ss2.at[step, i, way], self.rs2.at[step, i, way], on[k])

        def first_all(self, step, i, way):
            return all_of(self.parts[i][1].at[step, way], self.ss1.at[step, i, way],
                          self.rs1.at[step, i, way], next_device)

        def last_all(self, step, i, way):
            return all_of(self.parts[i][3].at[step, way], self.ss2.at[step, i, way],
                          self.rs2.at[step, i, way], next_device)

        def begin(self, step, i, multiply):
            for way in range(2):
                for m, col in enumerate(self.cols[i][way]):
                    block = fold(multiply(col).reshape(16, 8, 512)).astype(BF)
                    self.parts[i][0][step, way, :, :, :, m * 256:(m + 1) * 256] = block.reshape(4, 4, 16, 256)
                for n in range(3):
                    self.first(step, i, way, n).start()

        def middle(self, step, i):
            for way in range(2):
                self.first_all(step, i, way).wait_recv()
                total = self.share(step, i, way, 0)[...].astype(F32)
                for n in range(3):
                    total = total + self.parts[i][1][step, way, n].astype(F32)
                self.parts[i][2][step, way] = total.astype(BF)
                for n in range(3):
                    self.last(step, i, way, n).start()

        def end(self, step, i, way):
            self.last_all(step, i, way).wait_recv()
            total = self.parts[i][2][step, way, z if way == 0 else x].astype(F32)
            for n in range(3):
                total = total + self.parts[i][3][step, way, n].astype(F32)
            return total

        def drain(self):
            for step in range(2):
                for i in range(2):
                    for way in range(2):
                        self.first_all(step, i, way).wait_send()
                        self.last_all(step, i, way).wait_send()

    c_sum = Sum(
        c_cols,
        ((c_send1, c_recv1, c_send2, c_recv2), (c_tail1, c_tail2, c_tail3, c_tail4)),
        (ss_c1, rs_c1, ss_c2, rs_c2),
    )
    e_sum = Sum(
        e_cols,
        ((e_send1, e_recv1, e_send2, e_recv2), (e_tail1, e_tail2, e_tail3, e_tail4)),
        (ss_e1, rs_e1, ss_e2, rs_e2),
    )

    def begin_c(step, i):
        c_sum.begin(step, i, lambda col: jnp.dot(
            val_b[step], w_v[col], preferred_element_type=F32
        ))

    rows_in = (gath, gath_tail)

    def g_first(step, i, way, n):
        on = on_x if way == 0 else on_z
        block = rows_in[i].at[step, way, z, x]
        return copy_to(block, block, ss_g.at[step, i, way, 0], rs_g.at[step, i, way, 0], on[LINE[n]])

    def g_last(step, i, way, n):
        on = on_z if way == 0 else on_x
        block = rows_in[i].at[step, 0, z] if way == 0 else rows_in[i].at[step, 1, :, x]
        return copy_to(block, block, ss_g.at[step, i, way, 1], rs_g.at[step, i, way, 1], on[LINE[n]])

    def g_first_all(step, i, way):
        return all_of(rows_in[i].at[step, way, 0, pl.ds(0, 3)],
                      ss_g.at[step, i, way, 0], rs_g.at[step, i, way, 0], next_device)

    def g_last_all(step, i, way):
        return all_of(rows_in[i].at[step, way, pl.ds(0, 3)],
                      ss_g.at[step, i, way, 1], rs_g.at[step, i, way, 1], next_device)

    def hidden(step, i):
        for way in range(2):
            total = c_sum.end(step, i, way)
            for m, col in enumerate(c_cols[i][way]):
                own = x_in[step, :, pl.ds(pl.multiple_of(col * 512, 512), 512)].astype(F32)
                here = slice(m * 256, (m + 1) * 256)
                block = total[:, here] + fold(own)
                hid[step, col] = block
                rows_in[i][step, way, z, x, :, here] = block.astype(BF)
            for n in range(3):
                g_first(step, i, way, n).start()

    def gather(step, i):
        for way in range(2):
            g_first_all(step, i, way).wait_recv()
            for n in range(3):
                g_last(step, i, way, n).start()

    def expand(step, i):
        total = None
        squares = None
        for way in range(2):
            g_last_all(step, i, way).wait_recv()
            for m, col in enumerate(c_cols[i][way]):
                rows = rows_in[i][step, way, :, :, :, m * 256:(m + 1) * 256].reshape(16, 16, 256)
                a = unfold(rows.astype(F32)).reshape(128, 512)
                more = jnp.sum(a * a, axis=-1, keepdims=True)
                term = jnp.dot(a.astype(BF), up_v[col], preferred_element_type=F32)
                total = term if total is None else total + term
                squares = more if squares is None else squares + more
        if i == 0:
            acc[step] = total
            square[step] = squares
        else:
            v = (acc[step] + total) * lax.rsqrt((square[step] + squares) / D + EPSILON)
            act[step] = (v / (1.0 + jnp.exp(-v))).astype(BF)

    def begin_e(step, i):
        e_sum.begin(step, i, lambda col: jnp.dot(
            act[step], dn_v[:, col * 512:(col + 1) * 512], preferred_element_type=F32
        ))

    def finish(step, i):
        for way in range(2):
            total = e_sum.end(step, i, way)
            for m, col in enumerate(e_cols[i][way]):
                result = unfold(hid[step, col] + total[:, m * 256:(m + 1) * 256])
                out[step, :, col * 512:(col + 1) * 512] = result.astype(BF)

    def weights_near():
        w_up[1].wait_recv()
        w_dn[1].wait_recv()
        w_sib_up.start()
        w_sib_dn.start()
        ow_copy.wait()
        w_sib.wait_recv()
        w_sib_up.wait_recv()
        w_sib_dn.wait_recv()

    def weights_far():
        w_up2.wait_recv()
        w_dn2.wait_recv()
        w_sib_far.start()
        w_sib_far.wait_recv()

    w_up[0].wait_recv()
    w_up2.start()
    w_dn[0].wait_recv()
    w_dn2.start()
    for c in vu_copies:
        c.wait()
    values(0)
    weights_near()
    begin_c(0, 0)
    values(1)
    begin_c(1, 0)
    c_sum.middle(0, 0)
    weights_far()
    begin_c(0, 1)
    begin_c(1, 1)
    c_sum.middle(1, 0)
    hidden(0, 0)
    c_sum.middle(0, 1)
    c_sum.middle(1, 1)
    hidden(1, 0)
    hidden(0, 1)
    gather(0, 0)
    gather(0, 1)
    hidden(1, 1)
    gather(1, 0)
    up_copy.wait()
    expand(0, 0)
    gather(1, 1)
    expand(0, 1)
    dn_copy.wait()
    begin_e(0, 0)
    expand(1, 0)
    begin_e(0, 1)
    expand(1, 1)
    begin_e(1, 0)
    begin_e(1, 1)
    e_sum.middle(0, 0)
    e_sum.middle(0, 1)
    e_sum.middle(1, 0)
    e_sum.middle(1, 1)
    finish(0, 0)
    finish(0, 1)
    finish(1, 0)
    finish(1, 1)

    for c in (x_all, p_all, k_all, m_all):
        c.wait_send()

    def drain(i, carry):
        a_all(i // 2, i % 2).wait_send()
        return carry

    lax.fori_loop(0, 4, drain, 0)
    for c in w_up + w_dn + [w_sib, w_up2, w_dn2, w_sib_dn, w_sib_up, w_sib_far]:
        c.wait_send()
    c_sum.drain()
    e_sum.drain()
    for step in range(2):
        for i in range(2):
            for way in range(2):
                g_first_all(step, i, way).wait_send()
                g_last_all(step, i, way).wait_send()


def layer(lengths, inputs, frequency, queries, cache, down_latent, value_up, output_weight, up_weight, down_weight):
    vmem, hbm = pl.BlockSpec(memory_space=pltpu.VMEM), pl.BlockSpec(memory_space=pl.ANY)
    dma = pltpu.SemaphoreType.DMA
    scratch = [
        pltpu.VMEM((2, 8, D), BF),
        pltpu.VMEM((16, 64), F32),
        pltpu.VMEM((2, 8, WIDTH, 128), BF),
        pltpu.VMEM((8, WIDTH, CTX), BF),
        pltpu.VMEM((WIDTH, 256), BF),
        pltpu.VMEM((LAT, 1024), BF),
        pltpu.VMEM((8, 1024, 512), BF),
        pltpu.VMEM((8, 512, FF), BF),
        pltpu.VMEM((FF, D), BF),
        pltpu.VMEM((16, 2, 8, 256), BF),
        pltpu.VMEM((16, 16, WIDTH), BF),
        pltpu.VMEM((15, 16, WIDTH), BF),
        pltpu.VMEM((16, WIDTH), BF),
        pltpu.VMEM((16, LAT), F32),
        pltpu.VMEM((8, 128, LAT), F32),
        pltpu.VMEM((8, 256, 1), F32),
        pltpu.VMEM((8, 256, 1), F32),
        pltpu.VMEM((2, 4, 16, 16, LAT), BF),
        pltpu.VMEM((2, 4, 16, 16, LAT), BF),
        pltpu.VMEM((1024, 128), F32),
        pltpu.VMEM((2, 128, 1024), BF),
        pltpu.VMEM((2, 8, 16, 256), F32),
        pltpu.VMEM((2, 128, FF), F32),
        pltpu.VMEM((2, 128, 1), F32),
        pltpu.VMEM((2, 128, FF), BF),
    ]
    scratch += [
        pltpu.VMEM((16, 8, 128), F32),
        pltpu.VMEM((16, 8, 128), F32),
        pltpu.VMEM((16, 256), BF),
        pltpu.VMEM((16, 16, 256), BF),
        pltpu.VMEM((1024, 128), F32),
        pltpu.VMEM((1024, 128), F32),
    ]
    for gathers in (1, 0):
        for width in (768, 256):
            scratch += [
                pltpu.VMEM((2, 2, 4, 4, 16, width), BF),
                pltpu.VMEM((2, 2, 3, 4, 16, width), BF),
                pltpu.VMEM((2, 2, 4, 16, width), BF),
                pltpu.VMEM((2, 2, 3, 16, width), BF),
            ] + [pltpu.VMEM((2, 2, 4, 4, 16, width), BF)] * gathers
    scratch += [dma((8,)), dma((8,)), dma((7,)), dma((8,))]
    scratch += [dma] * 4 + [dma((2, 2))] * 2 + [dma] * 4 + [dma((10,))] * 2 + [dma((2, 2, 2, 2))] * 2
    scratch += [dma((2, 2, 2))] * 8
    return pl.pallas_call(
        kernel,
        out_shape=jax.ShapeDtypeStruct((2, 8, D), BF),
        in_specs=[pl.BlockSpec(memory_space=pltpu.SMEM)] + [hbm] * 9,
        out_specs=vmem,
        scratch_shapes=scratch,
        compiler_params=pltpu.CompilerParams(
            collective_id=0, has_side_effects=True, vmem_limit_bytes=60 * 1024 * 1024
        ),
    )(lengths, inputs, frequency, queries, cache, down_latent, value_up, output_weight, up_weight, down_weight)


def body(queries, latent_cache, lengths, inputs, down_latent, value_up, output_weight, up_weight, down_weight):
    half = ROPE_BASE ** (-np.arange(32, dtype=np.float32) / np.float32(32))
    frequency = np.tile(half.astype(np.float32), (16, 2))
    return layer(
        lengths, inputs, jnp.asarray(frequency),
        jnp.swapaxes(queries, 2, 3), jnp.swapaxes(latent_cache, 1, 2), down_latent.T,
        value_up, output_weight, up_weight.reshape(8, 512, FF), down_weight,
    )


def solution(mesh):
    return jax.shard_map(
        body,
        mesh=mesh,
        in_specs=(
            P(None, ("dp", "tp"), None, None),
            P(("dp", "tp"), None, None),
            P(("dp", "tp")),
            P(None, ("dp", "tp"), None),
            P("tp", None),
            P("tp", None, None),
            P("tp", "dp"),
            P(None, "tp"),
            P("tp", None),
        ),
        out_specs=P(None, ("dp", "tp"), None),
        check_vma=False,
    )
```

```python
import math

import jax
import jax.numpy as jnp
import numpy as np
from jax import lax
from jax.experimental import pallas as pl
from jax.experimental.pallas import tpu as pltpu
from jax.sharding import PartitionSpec as P

LAT = 512
WIDTH = 576
CTX = 512
D = 4096
FF = 640
EPSILON = 1e-06
SCORE_SCALE = 192.0 ** (-0.5)
ROPE_BASE = 10000.0
NEG = -1e30
BF = jnp.bfloat16
F32 = jnp.float32
MESH = pl.DeviceIdType.MESH

PLANE = (
    (0, 1), (0, 3), (1, 0), (3, 0), (2, 1), (1, 2), (2, 3), (3, 2),
    (2, 2), (1, 1), (3, 3), (1, 3), (3, 1), (0, 2), (2, 0),
)
LINE = (1, 3, 2)


def copy_to(src, dst, send_sem, recv_sem, device):
    return pltpu.make_async_remote_copy(
        src_ref=src, dst_ref=dst, send_sem=send_sem, recv_sem=recv_sem,
        device_id=device, device_id_type=MESH,
    )


def all_of(region, send_sem, recv_sem, device):
    return copy_to(region, region, send_sem, recv_sem, device)


def cos_sin(angles):
    turns = jnp.floor(angles * (0.5 / np.pi) + 0.5)
    rest = angles - turns * 6.28125
    rest = rest - turns * (2 * np.pi - 6.28125)
    square = rest * rest
    cosine = jnp.zeros_like(square)
    sine = jnp.zeros_like(square)
    for n in range(8, -1, -1):
        cosine = cosine * square + (-1.0) ** n / math.factorial(2 * n)
        sine = sine * square + (-1.0) ** n / math.factorial(2 * n + 1)
    return cosine, sine * rest


def kernel(
    lens, x_hbm, freq_hbm, q_hbm, c_hbm, dl_hbm, vu_hbm, ow_hbm, up_hbm, dn_hbm,
    out,
    x_in, freq_in, q_v, c_v, dl_v, vu_v, w_v, up_v, dn_v,
    xr, ps, pr, keys_b, keys_f, o_v, m_v, l_v,
    send_a, recv_a, val_f, val_b, hid, acc, square, act,
    mix_s, mix_r, key_s, key_r, keep_f, fresh_f,
    c_send1, c_recv1, c_send2, c_recv2, gath, c_tail1, c_tail2, c_tail3, c_tail4, gath_tail,
    e_send1, e_recv1, e_send2, e_recv2, e_tail1, e_tail2, e_tail3, e_tail4,
    sem_q, sem_c, sem_w, sem_vu,
    ss_x, rs_x, ss_p, rs_p, ss_a, rs_a, ss_m, rs_m, ss_k, rs_k, ss_w, rs_w, ss_g, rs_g,
    ss_c1, rs_c1, ss_c2, rs_c2, ss_e1, rs_e1, ss_e2, rs_e2,
):
    dp = lax.axis_index("dp")
    tp = lax.axis_index("tp")
    y, core = dp // 2, dp % 2
    z, x = tp // 4, tp % 4
    plane = [((z + dz) % 4) * 4 + (x + dx) % 4 for dz, dx in PLANE]
    on_x = {k: (dp, z * 4 + (x + k) % 4) for k in LINE}
    on_z = {k: (dp, ((z + k) % 4) * 4 + x) for k in LINE}
    next_device = (dp, plane[0])
    y_up, y_dn, y_far = (y + 1) % 4, (y + 3) % 4, (y + 2) % 4
    sibling = y * 2 + 1 - core

    barrier = pltpu.get_barrier_semaphore()
    partners = [(dp, t) for t in plane] + [
        (sibling, tp), (y_up * 2 + core, tp), (y_dn * 2 + core, tp)
    ]
    for device in partners:
        pl.semaphore_signal(barrier, inc=1, device_id=device, device_id_type=MESH)

    def q_copy(r):
        return pltpu.make_async_copy(q_hbm.at[:, r], q_v.at[:, r], sem_q.at[r])

    def c_copy(r):
        return pltpu.make_async_copy(c_hbm.at[r], c_v.at[r], sem_c.at[r])

    dl_copy = pltpu.make_async_copy(dl_hbm, dl_v, sem_w.at[0])
    ow_copy = pltpu.make_async_copy(ow_hbm, w_v.at[dp], sem_w.at[1])
    up_copy = pltpu.make_async_copy(up_hbm, up_v, sem_w.at[2])
    dn_copy = pltpu.make_async_copy(dn_hbm, dn_v, sem_w.at[3])
    x_copy = pltpu.make_async_copy(x_hbm, x_in, sem_w.at[4])
    freq_copy = pltpu.make_async_copy(freq_hbm, freq_in, sem_w.at[5])
    vu_copies = [
        pltpu.make_async_copy(vu_hbm.at[h], vu_v.at[:, pl.ds(h * 128, 128)], sem_vu.at[h])
        for h in range(8)
    ]
    x_copy.start()
    for r in range(2):
        q_copy(r).start()
        c_copy(r).start()
    dl_copy.start()

    pl.semaphore_wait(barrier, len(partners))

    def x_slice(t):
        return x_hbm.at[:, :, pl.ds(pl.multiple_of(t * 256, 256), 256)]

    x_copies = [
        copy_to(x_slice(t), xr.at[tp], ss_x, rs_x, (dp, t))
        for k, t in enumerate(plane)
    ]
    for c in x_copies:
        c.start()
    x_all = all_of(xr.at[pl.ds(0, 15)], ss_x, rs_x, next_device)
    for r in range(2, 8):
        q_copy(r).start()
        c_copy(r).start()
    freq_copy.start()
    x_own = pltpu.make_async_copy(x_slice(tp), xr.at[tp], sem_w.at[6])
    x_own.start()

    lo, hi = pl.ds(0, 512), pl.ds(512, 512)
    up_dev, dn_dev, sib_dev = (y_up * 2 + core, tp), (y_dn * 2 + core, tp), (sibling, tp)
    w_up = [
        copy_to(ow_hbm.at[s], w_v.at[dp, s], ss_w.at[i], rs_w.at[i], up_dev)
        for i, s in enumerate((lo, hi))
    ]
    w_dn = [
        copy_to(ow_hbm.at[s], w_v.at[dp, s], ss_w.at[2 + i], rs_w.at[2 + i], dn_dev)
        for i, s in enumerate((hi, lo))
    ]
    w_sib = copy_to(ow_hbm, w_v.at[dp], ss_w.at[4], rs_w.at[4], sib_dev)
    from_dn, from_up, from_far = y_dn * 2 + core, y_up * 2 + core, y_far * 2 + core
    w_up2 = copy_to(w_v.at[from_dn, lo], w_v.at[from_dn, lo], ss_w.at[5], rs_w.at[5], up_dev)
    w_dn2 = copy_to(w_v.at[from_up, hi], w_v.at[from_up, hi], ss_w.at[6], rs_w.at[6], dn_dev)
    w_sib_dn = [
        copy_to(w_v.at[from_dn, s], w_v.at[from_dn, s], ss_w.at[7 + i], rs_w.at[7 + i], sib_dev)
        for i, s in enumerate((lo, hi))
    ]
    w_sib_up = [
        copy_to(w_v.at[from_up, s], w_v.at[from_up, s], ss_w.at[10 + i], rs_w.at[10 + i], sib_dev)
        for i, s in enumerate((hi, lo))
    ]
    w_sib_far = copy_to(w_v.at[from_far], w_v.at[from_far], ss_w.at[9], rs_w.at[9], sib_dev)
    for c in (w_up[0], w_dn[0], w_up[1], w_dn[1], w_sib):
        c.start()
    ow_copy.start()

    def a_copies(step, g):
        rows = pl.ds(2 * g, 2)
        return [
            copy_to(send_a.at[step, rows, t], recv_a.at[step, rows, tp],
                    ss_a.at[step, g], rs_a.at[step, g], (dp, t))
            for t in plane
        ]

    def a_pair(pair):
        return [
            copy_to(send_a.at[0, pair, t], recv_a.at[0, pair, tp],
                    ss_a.at[0, pair // 2], rs_a.at[0, pair // 2], (dp, t))
            for t in plane
        ]

    def a_all(step, g):
        return all_of(recv_a.at[step, pl.ds(2 * g, 2), pl.ds(0, 15)],
                      ss_a.at[step, g], rs_a.at[step, g], next_device)

    def attend_row(r):
        q_copy(r).wait()
        c_copy(r).wait()
        q = jnp.concatenate([q_v[0, r], q_v[1, r]], axis=1)
        k = c_v[r]
        s = lax.dot_general(
            q, k, (((0,), (0,)), ((), ())), preferred_element_type=F32
        ) * SCORE_SCALE
        position = lax.broadcasted_iota(jnp.int32, (1, CTX), 1)
        s = jnp.where(position < lens[r], s, NEG)
        m = jnp.max(s, axis=-1, keepdims=True)
        p = jnp.exp(s - m)
        total = jnp.sum(p, axis=-1, keepdims=True)
        l_v[r] = total
        m_v[r] = m
        o = lax.dot_general(
            p.astype(BF), k[:LAT], (((1,), (1,)), ((), ())), preferred_element_type=F32
        )
        o_v[r] = o[128:]
        return (o[:128] * (1.0 / total[:128])).reshape(16, 8, LAT)

    def attend_pair(pair, carry):
        both = [attend_row(2 * pair), attend_row(2 * pair + 1)]
        send_a[0, pair] = jnp.concatenate(both, axis=1).astype(BF)
        recv_a[0, pair, tp] = send_a[0, pair, tp]
        return carry

    lax.fori_loop(0, 1, attend_pair, 0)
    for c in a_pair(0):
        c.start()

    for c in vu_copies:
        c.start()
    up_copy.start()
    dn_copy.start()

    dl_copy.wait()
    x_own.wait()
    x_all.wait_recv()
    partial = lax.dot_general(
        xr[...].astype(F32).reshape(256, 256).astype(BF), dl_v[...], (((1,), (1,)), ((), ())),
        preferred_element_type=F32,
    )
    ps[...] = partial.astype(BF).reshape(16, 16, WIDTH)
    p_copies = [
        copy_to(ps.at[t], pr.at[k], ss_p, rs_p, (dp, t))
        for k, t in enumerate(plane)
    ]
    for c in p_copies:
        c.start()
    p_all = all_of(pr, ss_p, rs_p, next_device)

    def attend_and_send(pair, carry):
        attend_pair(pair, carry)
        for c in a_pair(pair):
            c.start()
        return carry

    lax.fori_loop(1, 4, attend_and_send, 0)

    freq_copy.wait()
    x_copy.wait()
    x0 = jnp.concatenate([x_in[0].astype(F32), x_in[1].astype(F32)], axis=0)
    x_scale = lax.rsqrt(jnp.mean(x0 * x0, axis=-1, keepdims=True) + EPSILON)
    p_all.wait_recv()
    comp = ps[tp].astype(F32)
    for k in range(15):
        comp = comp + pr[k].astype(F32)
    comp = comp * x_scale
    lat = comp[:, :LAT]
    lat = lat * lax.rsqrt(jnp.mean(lat * lat, axis=-1, keepdims=True) + EPSILON)
    rope = comp[:, LAT:]
    swapped = jnp.concatenate([rope[:, 32:], rope[:, :32]], axis=-1)
    row = lax.broadcasted_iota(jnp.int32, (16, 64), 0)
    position = row // 8
    for r in range(8):
        position = position + jnp.where(row % 8 == r, lens[r], 0)
    cosine, sine = cos_sin(position.astype(F32) * freq_in[...])
    first = lax.broadcasted_iota(jnp.int32, (16, 64), 1) < 32
    rotated = rope * cosine + swapped * jnp.where(first, -sine, sine)
    keys_b[:, :LAT] = lat.astype(BF)
    keys_b[:, LAT:] = rotated.astype(BF)
    keys_f[...] = lat.astype(BF).astype(F32)

    key_s[...] = jnp.concatenate([lat[:8, :256], lat[:8, 256:]], axis=0).astype(BF)
    key_r[tp] = key_s[...]
    k_copies = [
        copy_to(key_s, key_r.at[tp], ss_k, rs_k, (dp, t)) for k, t in enumerate(plane)
    ]
    for c in k_copies:
        c.start()
    k_all = all_of(key_r.at[pl.ds(0, 15)], ss_k, rs_k, next_device)

    def fresh_scores(step, r):
        fresh = jnp.dot(keys_b[...], q_v[step, r], preferred_element_type=F32).T * SCORE_SCALE
        lane = lax.broadcasted_iota(jnp.int32, (128, 16), 1)
        s0 = jnp.sum(jnp.where(lane == r, fresh, 0.0), axis=-1, keepdims=True)
        s1 = jnp.sum(jnp.where(lane == r + 8, fresh, 0.0), axis=-1, keepdims=True)
        return s0, s1

    def mix_row(r, mix):
        s0, _ = fresh_scores(0, r)
        m_old = m_v[r, :128]
        m = jnp.maximum(m_old, s0)
        cached = jnp.exp(m_old - m) * l_v[r, :128]
        p0 = jnp.exp(s0 - m)
        inverse = 1.0 / (cached + p0)
        lane = lax.broadcasted_iota(jnp.int32, (128, 128), 1)
        mix = jnp.where(lane == r, cached * inverse, mix)
        return jnp.where(lane == r + 8, p0 * inverse, mix)

    mix = lax.fori_loop(0, 8, mix_row, jnp.zeros((128, 128), F32))
    mix_s[...] = mix.reshape(16, 8, 128)
    mix_r[tp] = mix_s[tp]
    m_copies = [
        copy_to(mix_s.at[t], mix_r.at[tp], ss_m, rs_m, (dp, t))
        for k, t in enumerate(plane)
    ]
    for c in m_copies:
        c.start()
    m_all = all_of(mix_r.at[pl.ds(0, 15)], ss_m, rs_m, next_device)

    def finish_row(r):
        s0, s1 = fresh_scores(1, r)
        m_old = m_v[r, 128:]
        m = jnp.maximum(jnp.maximum(m_old, s0), s1)
        keep = jnp.exp(m_old - m)
        p0 = jnp.exp(s0 - m)
        p1 = jnp.exp(s1 - m)
        inverse = 1.0 / (keep * l_v[r, 128:] + p0 + p1)
        k0 = keys_f[pl.ds(r, 1), :]
        k1 = keys_f[pl.ds(r + 8, 1), :]
        o = o_v[r] * (keep * inverse) + (p0 * inverse) * k0 + (p1 * inverse) * k1
        return o.reshape(16, 8, LAT)

    def finish_four(g, carry):
        for j in range(2):
            pair = 2 * g + j
            both = [finish_row(2 * pair), finish_row(2 * pair + 1)]
            send_a[1, pair] = jnp.concatenate(both, axis=1).astype(BF)
            recv_a[1, pair, tp] = send_a[1, pair, tp]
        for c in a_copies(1, g):
            c.start()
        return carry

    lax.fori_loop(0, 2, finish_four, 0)

    def values(step):
        def four(g, carry):
            a_all(step, g).wait_recv()
            head = lax.broadcasted_iota(jnp.int32, (8, 128), 0)[None]
            for j in range(2):
                pair = 2 * g + j
                a = recv_a[step, pair].reshape(256, LAT)
                full = jnp.dot(a, vu_v[...], preferred_element_type=F32)
                full = full.reshape(32, 8, 1024)
                own = jnp.where(head == 0, full[:, :, :128], 0.0)
                for h in range(1, 8):
                    own = jnp.where(head == h, full[:, :, h * 128:(h + 1) * 128], own)
                for b in range(32):
                    at = pl.multiple_of((b // 2) * 64 + (2 * pair + b % 2) * 8, 8)
                    val_f[pl.ds(at, 8), :] = own[b]
            return carry

        lax.fori_loop(0, 2, four, 0)
        if step == 0:
            k_all.wait_recv()
            m_all.wait_recv()

            def spread(src, carry):
                tile = mix_r[src]
                for r in range(8):
                    at = pl.ds(pl.multiple_of(src * 64 + r * 8, 8), 8)
                    keep_f[at, :] = jnp.broadcast_to(tile[:, r:r + 1], (8, 128))
                    fresh_f[at, :] = jnp.broadcast_to(tile[:, r + 8:r + 9], (8, 128))
                return carry

            lax.fori_loop(0, 16, spread, 0)
            keys = key_r[...].astype(F32)
            keys = jnp.concatenate([keys[:, :8], keys[:, 8:]], axis=2).reshape(128, LAT).astype(BF)
            projected = jnp.dot(keys, vu_v[...], preferred_element_type=F32)
        for h in range(8):
            cols = slice(h * 128, (h + 1) * 128)
            own = pl.ds(h, 128, stride=8)
            if step == 0:
                mixed = keep_f[own, :] * val_f[own, :] + fresh_f[own, :] * projected[:, cols]
                val_b[0, :, cols] = mixed.astype(BF)
            else:
                val_b[1, :, cols] = val_f[own, :].astype(BF)

    def ways(order):
        return ((order[0:3], order[3:6]), (order[6:7], order[7:8]))

    c_cols = ways([b * 2 + c for b in (y, y_up, y_dn, y_far) for c in range(2)])
    e_cols = ways(list(range(8)))

    def fold(a):
        return jnp.concatenate([a[..., :256], a[..., 256:]], axis=-2)

    def unfold(a):
        return jnp.concatenate([a[..., :8, :], a[..., 8:, :]], axis=-1)

    class Sum:
        def __init__(self, cols, parts, sems):
            self.cols, self.parts = cols, parts
            self.ss1, self.rs1, self.ss2, self.rs2 = sems

        def share(self, step, i, way, k):
            send1 = self.parts[i][0]
            if way == 0:
                return send1.at[step, 0, :, (x + k) % 4]
            return send1.at[step, 1, (z + k) % 4]

        def first(self, step, i, way, n):
            on = on_x if way == 0 else on_z
            k = LINE[n]
            return copy_to(self.share(step, i, way, k), self.parts[i][1].at[step, way, n],
                           self.ss1.at[step, i, way], self.rs1.at[step, i, way], on[k])

        def last(self, step, i, way, n):
            on, here = (on_z, z) if way == 0 else (on_x, x)
            k = LINE[n]
            return copy_to(self.parts[i][2].at[step, way, (here + k) % 4], self.parts[i][3].at[step, way, n],
                           self.ss2.at[step, i, way], self.rs2.at[step, i, way], on[k])

        def first_all(self, step, i, way):
            return all_of(self.parts[i][1].at[step, way], self.ss1.at[step, i, way],
                          self.rs1.at[step, i, way], next_device)

        def last_all(self, step, i, way):
            return all_of(self.parts[i][3].at[step, way], self.ss2.at[step, i, way],
                          self.rs2.at[step, i, way], next_device)

        def begin(self, step, i, multiply):
            for way in range(2):
                for m, col in enumerate(self.cols[i][way]):
                    block = fold(multiply(col).reshape(16, 8, 512)).astype(BF)
                    self.parts[i][0][step, way, :, :, :, m * 256:(m + 1) * 256] = block.reshape(4, 4, 16, 256)
                for n in range(3):
                    self.first(step, i, way, n).start()

        def middle(self, step, i):
            for way in range(2):
                self.first_all(step, i, way).wait_recv()
                total = self.share(step, i, way, 0)[...].astype(F32)
                for n in range(3):
                    total = total + self.parts[i][1][step, way, n].astype(F32)
                self.parts[i][2][step, way] = total.astype(BF)
                for n in range(3):
                    self.last(step, i, way, n).start()

        def end(self, step, i, way):
            self.last_all(step, i, way).wait_recv()
            total = self.parts[i][2][step, way, z if way == 0 else x].astype(F32)
            for n in range(3):
                total = total + self.parts[i][3][step, way, n].astype(F32)
            return total

        def drain(self):
            for step in range(2):
                for i in range(2):
                    for way in range(2):
                        self.first_all(step, i, way).wait_send()
                        self.last_all(step, i, way).wait_send()

    c_sum = Sum(
        c_cols,
        ((c_send1, c_recv1, c_send2, c_recv2), (c_tail1, c_tail2, c_tail3, c_tail4)),
        (ss_c1, rs_c1, ss_c2, rs_c2),
    )
    e_sum = Sum(
        e_cols,
        ((e_send1, e_recv1, e_send2, e_recv2), (e_tail1, e_tail2, e_tail3, e_tail4)),
        (ss_e1, rs_e1, ss_e2, rs_e2),
    )

    def begin_c(step, i):
        c_sum.begin(step, i, lambda col: jnp.dot(
            val_b[step], w_v[col], preferred_element_type=F32
        ))

    rows_in = (gath, gath_tail)

    def g_first(step, i, way, n):
        on = on_x if way == 0 else on_z
        block = rows_in[i].at[step, way, z, x]
        return copy_to(block, block, ss_g.at[step, i, way, 0], rs_g.at[step, i, way, 0], on[LINE[n]])

    def g_last(step, i, way, n):
        on = on_z if way == 0 else on_x
        block = rows_in[i].at[step, 0, z] if way == 0 else rows_in[i].at[step, 1, :, x]
        return copy_to(block, block, ss_g.at[step, i, way, 1], rs_g.at[step, i, way, 1], on[LINE[n]])

    def g_first_all(step, i, way):
        return all_of(rows_in[i].at[step, way, 0, pl.ds(0, 3)],
                      ss_g.at[step, i, way, 0], rs_g.at[step, i, way, 0], next_device)

    def g_last_all(step, i, way):
        return all_of(rows_in[i].at[step, way, pl.ds(0, 3)],
                      ss_g.at[step, i, way, 1], rs_g.at[step, i, way, 1], next_device)

    def hidden(step, i):
        for way in range(2):
            total = c_sum.end(step, i, way)
            for m, col in enumerate(c_cols[i][way]):
                own = x_in[step, :, pl.ds(pl.multiple_of(col * 512, 512), 512)].astype(F32)
                here = slice(m * 256, (m + 1) * 256)
                block = total[:, here] + fold(own)
                hid[step, col] = block
                rows_in[i][step, way, z, x, :, here] = block.astype(BF)
            for n in range(3):
                g_first(step, i, way, n).start()

    def gather(step, i):
        for way in range(2):
            g_first_all(step, i, way).wait_recv()
            for n in range(3):
                g_last(step, i, way, n).start()

    def expand(step, i):
        total = None
        squares = None
        for way in range(2):
            g_last_all(step, i, way).wait_recv()
            for m, col in enumerate(c_cols[i][way]):
                rows = rows_in[i][step, way, :, :, :, m * 256:(m + 1) * 256].reshape(16, 16, 256)
                a = unfold(rows.astype(F32)).reshape(128, 512)
                more = jnp.sum(a * a, axis=-1, keepdims=True)
                term = jnp.dot(a.astype(BF), up_v[col], preferred_element_type=F32)
                total = term if total is None else total + term
                squares = more if squares is None else squares + more
        if i == 0:
            acc[step] = total
            square[step] = squares
        else:
            v = (acc[step] + total) * lax.rsqrt((square[step] + squares) / D + EPSILON)
            act[step] = (v / (1.0 + jnp.exp(-v))).astype(BF)

    def begin_e(step, i):
        e_sum.begin(step, i, lambda col: jnp.dot(
            act[step], dn_v[:, col * 512:(col + 1) * 512], preferred_element_type=F32
        ))

    def finish(step, i):
        for way in range(2):
            total = e_sum.end(step, i, way)
            for m, col in enumerate(e_cols[i][way]):
                result = unfold(hid[step, col] + total[:, m * 256:(m + 1) * 256])
                out[step, :, col * 512:(col + 1) * 512] = result.astype(BF)

    def weights_near():
        w_up[1].wait_recv()
        w_sib_dn[1].start()
        w_dn[1].wait_recv()
        w_sib_up[1].start()
        ow_copy.wait()
        w_sib.wait_recv()
        for c in w_sib_up + w_sib_dn:
            c.wait_recv()

    def weights_far():
        w_up2.wait_recv()
        w_dn2.wait_recv()
        w_sib_far.start()
        w_sib_far.wait_recv()

    w_up[0].wait_recv()
    w_up2.start()
    w_sib_dn[0].start()
    w_dn[0].wait_recv()
    w_dn2.start()
    w_sib_up[0].start()
    for c in vu_copies:
        c.wait()
    values(0)
    weights_near()
    begin_c(0, 0)
    values(1)
    begin_c(1, 0)
    c_sum.middle(0, 0)
    weights_far()
    begin_c(0, 1)
    begin_c(1, 1)
    c_sum.middle(1, 0)
    hidden(0, 0)
    c_sum.middle(0, 1)
    c_sum.middle(1, 1)
    hidden(1, 0)
    hidden(0, 1)
    gather(0, 0)
    gather(0, 1)
    hidden(1, 1)
    gather(1, 0)
    up_copy.wait()
    expand(0, 0)
    gather(1, 1)
    expand(0, 1)
    dn_copy.wait()
    begin_e(0, 0)
    expand(1, 0)
    begin_e(0, 1)
    expand(1, 1)
    begin_e(1, 0)
    begin_e(1, 1)
    e_sum.middle(0, 0)
    e_sum.middle(0, 1)
    e_sum.middle(1, 0)
    e_sum.middle(1, 1)
    finish(0, 0)
    finish(0, 1)
    finish(1, 0)
    finish(1, 1)

    for c in (x_all, p_all, k_all, m_all):
        c.wait_send()

    def drain(i, carry):
        a_all(i // 2, i % 2).wait_send()
        return carry

    lax.fori_loop(0, 4, drain, 0)
    for c in w_up + w_dn + w_sib_dn + w_sib_up + [w_sib, w_up2, w_dn2, w_sib_far]:
        c.wait_send()
    c_sum.drain()
    e_sum.drain()
    for step in range(2):
        for i in range(2):
            for way in range(2):
                g_first_all(step, i, way).wait_send()
                g_last_all(step, i, way).wait_send()


def layer(lengths, inputs, frequency, queries, cache, down_latent, value_up, output_weight, up_weight, down_weight):
    vmem, hbm = pl.BlockSpec(memory_space=pltpu.VMEM), pl.BlockSpec(memory_space=pl.ANY)
    dma = pltpu.SemaphoreType.DMA
    scratch = [
        pltpu.VMEM((2, 8, D), BF),
        pltpu.VMEM((16, 64), F32),
        pltpu.VMEM((2, 8, WIDTH, 128), BF),
        pltpu.VMEM((8, WIDTH, CTX), BF),
        pltpu.VMEM((WIDTH, 256), BF),
        pltpu.VMEM((LAT, 1024), BF),
        pltpu.VMEM((8, 1024, 512), BF),
        pltpu.VMEM((8, 512, FF), BF),
        pltpu.VMEM((FF, D), BF),
        pltpu.VMEM((16, 2, 8, 256), BF),
        pltpu.VMEM((16, 16, WIDTH), BF),
        pltpu.VMEM((15, 16, WIDTH), BF),
        pltpu.VMEM((16, WIDTH), BF),
        pltpu.VMEM((16, LAT), F32),
        pltpu.VMEM((8, 128, LAT), F32),
        pltpu.VMEM((8, 256, 1), F32),
        pltpu.VMEM((8, 256, 1), F32),
        pltpu.VMEM((2, 4, 16, 16, LAT), BF),
        pltpu.VMEM((2, 4, 16, 16, LAT), BF),
        pltpu.VMEM((1024, 128), F32),
        pltpu.VMEM((2, 128, 1024), BF),
        pltpu.VMEM((2, 8, 16, 256), F32),
        pltpu.VMEM((2, 128, FF), F32),
        pltpu.VMEM((2, 128, 1), F32),
        pltpu.VMEM((2, 128, FF), BF),
    ]
    scratch += [
        pltpu.VMEM((16, 8, 128), F32),
        pltpu.VMEM((16, 8, 128), F32),
        pltpu.VMEM((16, 256), BF),
        pltpu.VMEM((16, 16, 256), BF),
        pltpu.VMEM((1024, 128), F32),
        pltpu.VMEM((1024, 128), F32),
    ]
    for gathers in (1, 0):
        for width in (768, 256):
            scratch += [
                pltpu.VMEM((2, 2, 4, 4, 16, width), BF),
                pltpu.VMEM((2, 2, 3, 4, 16, width), BF),
                pltpu.VMEM((2, 2, 4, 16, width), BF),
                pltpu.VMEM((2, 2, 3, 16, width), BF),
            ] + [pltpu.VMEM((2, 2, 4, 4, 16, width), BF)] * gathers
    scratch += [dma((8,)), dma((8,)), dma((7,)), dma((8,))]
    scratch += [dma] * 4 + [dma((2, 2))] * 2 + [dma] * 4 + [dma((12,))] * 2 + [dma((2, 2, 2, 2))] * 2
    scratch += [dma((2, 2, 2))] * 8
    return pl.pallas_call(
        kernel,
        out_shape=jax.ShapeDtypeStruct((2, 8, D), BF),
        in_specs=[pl.BlockSpec(memory_space=pltpu.SMEM)] + [hbm] * 9,
        out_specs=vmem,
        scratch_shapes=scratch,
        compiler_params=pltpu.CompilerParams(
            collective_id=0, has_side_effects=True, vmem_limit_bytes=60 * 1024 * 1024
        ),
    )(lengths, inputs, frequency, queries, cache, down_latent, value_up, output_weight, up_weight, down_weight)


def body(queries, latent_cache, lengths, inputs, down_latent, value_up, output_weight, up_weight, down_weight):
    half = ROPE_BASE ** (-np.arange(32, dtype=np.float32) / np.float32(32))
    frequency = np.tile(half.astype(np.float32), (16, 2))
    return layer(
        lengths, inputs, jnp.asarray(frequency),
        jnp.swapaxes(queries, 2, 3), jnp.swapaxes(latent_cache, 1, 2), down_latent.T,
        value_up, output_weight, up_weight.reshape(8, 512, FF), down_weight,
    )


def solution(mesh):
    return jax.shard_map(
        body,
        mesh=mesh,
        in_specs=(
            P(None, ("dp", "tp"), None, None),
            P(("dp", "tp"), None, None),
            P(("dp", "tp")),
            P(None, ("dp", "tp"), None),
            P("tp", None),
            P("tp", None, None),
            P("tp", "dp"),
            P(None, "tp"),
            P("tp", None),
        ),
        out_specs=P(None, ("dp", "tp"), None),
        check_vma=False,
    )
```

```python
import math

import jax
import jax.numpy as jnp
import numpy as np
from jax import lax
from jax.experimental import pallas as pl
from jax.experimental.pallas import tpu as pltpu
from jax.sharding import PartitionSpec as P

LAT = 512
WIDTH = 576
CTX = 512
D = 4096
FF = 640
EPSILON = 1e-06
SCORE_SCALE = 192.0 ** (-0.5)
ROPE_BASE = 10000.0
NEG = -1e30
BF = jnp.bfloat16
F32 = jnp.float32
MESH = pl.DeviceIdType.MESH

PLANE = (
    (0, 1), (0, 3), (1, 0), (3, 0), (2, 1), (1, 2), (2, 3), (3, 2),
    (2, 2), (1, 1), (3, 3), (1, 3), (3, 1), (0, 2), (2, 0),
)
LINE = (1, 3, 2)


def copy_to(src, dst, send_sem, recv_sem, device):
    return pltpu.make_async_remote_copy(
        src_ref=src, dst_ref=dst, send_sem=send_sem, recv_sem=recv_sem,
        device_id=device, device_id_type=MESH,
    )


def all_of(region, send_sem, recv_sem, device):
    return copy_to(region, region, send_sem, recv_sem, device)


def cos_sin(angles):
    turns = jnp.floor(angles * (0.5 / np.pi) + 0.5)
    rest = angles - turns * 6.28125
    rest = rest - turns * (2 * np.pi - 6.28125)
    square = rest * rest
    cosine = jnp.zeros_like(square)
    sine = jnp.zeros_like(square)
    for n in range(8, -1, -1):
        cosine = cosine * square + (-1.0) ** n / math.factorial(2 * n)
        sine = sine * square + (-1.0) ** n / math.factorial(2 * n + 1)
    return cosine, sine * rest


def kernel(
    lens, x_hbm, freq_hbm, q_hbm, c_hbm, dl_hbm, vu_hbm, ow_hbm, up_hbm, dn_hbm,
    out,
    x_in, freq_in, q_v, c_v, dl_v, vu_v, w_v, up_v, dn_v,
    xr, ps, pr, keys_b, keys_f, o_v, m_v, l_v,
    send_a, recv_a, val_f, val_b, hid, acc, square, act,
    mix_s, mix_r, key_s, key_r, keep_f, fresh_f,
    c_send1, c_recv1, c_send2, c_recv2, gath, c_tail1, c_tail2, c_tail3, c_tail4, gath_tail,
    e_send1, e_recv1, e_send2, e_recv2, e_tail1, e_tail2, e_tail3, e_tail4,
    sem_q, sem_c, sem_w, sem_vu,
    ss_x, rs_x, ss_p, rs_p, ss_a, rs_a, ss_m, rs_m, ss_k, rs_k, ss_w, rs_w, ss_g, rs_g,
    ss_c1, rs_c1, ss_c2, rs_c2, ss_e1, rs_e1, ss_e2, rs_e2,
):
    dp = lax.axis_index("dp")
    tp = lax.axis_index("tp")
    y, core = dp // 2, dp % 2
    z, x = tp // 4, tp % 4
    plane = [((z + dz) % 4) * 4 + (x + dx) % 4 for dz, dx in PLANE]
    on_x = {k: (dp, z * 4 + (x + k) % 4) for k in LINE}
    on_z = {k: (dp, ((z + k) % 4) * 4 + x) for k in LINE}
    next_device = (dp, plane[0])
    y_up, y_dn, y_far = (y + 1) % 4, (y + 3) % 4, (y + 2) % 4
    sibling = y * 2 + 1 - core

    barrier = pltpu.get_barrier_semaphore()
    partners = [(dp, t) for t in plane] + [
        (sibling, tp), (y_up * 2 + core, tp), (y_dn * 2 + core, tp)
    ]
    for device in partners:
        pl.semaphore_signal(barrier, inc=1, device_id=device, device_id_type=MESH)

    def q_copy(r):
        return pltpu.make_async_copy(q_hbm.at[:, r], q_v.at[:, r], sem_q.at[r])

    def c_copy(r):
        return pltpu.make_async_copy(c_hbm.at[r], c_v.at[r], sem_c.at[r])

    dl_copy = pltpu.make_async_copy(dl_hbm, dl_v, sem_w.at[0])
    ow_copy = pltpu.make_async_copy(ow_hbm, w_v.at[dp], sem_w.at[1])
    up_copy = pltpu.make_async_copy(up_hbm, up_v, sem_w.at[2])
    dn_copy = pltpu.make_async_copy(dn_hbm, dn_v, sem_w.at[3])
    x_copy = pltpu.make_async_copy(x_hbm, x_in, sem_w.at[4])
    freq_copy = pltpu.make_async_copy(freq_hbm, freq_in, sem_w.at[5])
    vu_copies = [
        pltpu.make_async_copy(vu_hbm.at[h], vu_v.at[:, pl.ds(h * 128, 128)], sem_vu.at[h])
        for h in range(8)
    ]
    x_copy.start()
    for r in range(2):
        q_copy(r).start()
        c_copy(r).start()
    dl_copy.start()

    pl.semaphore_wait(barrier, len(partners))

    def x_slice(t):
        return x_hbm.at[:, pl.ds(pl.multiple_of(t * 256, 256), 256)]

    x_copies = [
        copy_to(x_slice(t), xr.at[tp], ss_x, rs_x, (dp, t))
        for k, t in enumerate(plane)
    ]
    for c in x_copies:
        c.start()
    x_all = all_of(xr.at[pl.ds(0, 15)], ss_x, rs_x, next_device)
    for r in range(2, 8):
        q_copy(r).start()
        c_copy(r).start()
    freq_copy.start()
    x_own = pltpu.make_async_copy(x_slice(tp), xr.at[tp], sem_w.at[6])
    x_own.start()

    lo, hi = pl.ds(0, 512), pl.ds(512, 512)
    up_dev, dn_dev, sib_dev = (y_up * 2 + core, tp), (y_dn * 2 + core, tp), (sibling, tp)
    w_up = [
        copy_to(ow_hbm.at[s], w_v.at[dp, s], ss_w.at[i], rs_w.at[i], up_dev)
        for i, s in enumerate((lo, hi))
    ]
    w_dn = [
        copy_to(ow_hbm.at[s], w_v.at[dp, s], ss_w.at[2 + i], rs_w.at[2 + i], dn_dev)
        for i, s in enumerate((hi, lo))
    ]
    w_sib = copy_to(ow_hbm, w_v.at[dp], ss_w.at[4], rs_w.at[4], sib_dev)
    from_dn, from_up, from_far = y_dn * 2 + core, y_up * 2 + core, y_far * 2 + core
    w_up2 = copy_to(w_v.at[from_dn, lo], w_v.at[from_dn, lo], ss_w.at[5], rs_w.at[5], up_dev)
    w_dn2 = copy_to(w_v.at[from_up, hi], w_v.at[from_up, hi], ss_w.at[6], rs_w.at[6], dn_dev)
    w_sib_dn = [
        copy_to(w_v.at[from_dn, s], w_v.at[from_dn, s], ss_w.at[7 + i], rs_w.at[7 + i], sib_dev)
        for i, s in enumerate((lo, hi))
    ]
    w_sib_up = [
        copy_to(w_v.at[from_up, s], w_v.at[from_up, s], ss_w.at[10 + i], rs_w.at[10 + i], sib_dev)
        for i, s in enumerate((hi, lo))
    ]
    w_sib_far = copy_to(w_v.at[from_far], w_v.at[from_far], ss_w.at[9], rs_w.at[9], sib_dev)
    for c in (w_up[0], w_dn[0], w_up[1], w_dn[1], w_sib):
        c.start()
    ow_copy.start()

    def a_copies(step, g):
        rows = pl.ds(2 * g, 2)
        return [
            copy_to(send_a.at[step, rows, t], recv_a.at[step, rows, tp],
                    ss_a.at[step, g], rs_a.at[step, g], (dp, t))
            for t in plane
        ]

    def a_pair(pair):
        return [
            copy_to(send_a.at[0, pair, t], recv_a.at[0, pair, tp],
                    ss_a.at[0, pair // 2], rs_a.at[0, pair // 2], (dp, t))
            for t in plane
        ]

    def a_all(step, g):
        return all_of(recv_a.at[step, pl.ds(2 * g, 2), pl.ds(0, 15)],
                      ss_a.at[step, g], rs_a.at[step, g], next_device)

    def attend_row(r):
        q_copy(r).wait()
        c_copy(r).wait()
        q = jnp.concatenate([q_v[0, r], q_v[1, r]], axis=1)
        k = c_v[r]
        s = lax.dot_general(
            q, k, (((0,), (0,)), ((), ())), preferred_element_type=F32
        ) * SCORE_SCALE
        position = lax.broadcasted_iota(jnp.int32, (1, CTX), 1)
        s = jnp.where(position < lens[r], s, NEG)
        m = jnp.max(s, axis=-1, keepdims=True)
        p = jnp.exp(s - m)
        total = jnp.sum(p, axis=-1, keepdims=True)
        l_v[r] = total
        m_v[r] = m
        o = lax.dot_general(
            p.astype(BF), k[:LAT], (((1,), (1,)), ((), ())), preferred_element_type=F32
        )
        o_v[r] = o[128:]
        return (o[:128] * (1.0 / total[:128])).reshape(16, 8, LAT)

    def attend_pair(pair, carry):
        both = [attend_row(2 * pair), attend_row(2 * pair + 1)]
        send_a[0, pair] = jnp.concatenate(both, axis=1).astype(BF)
        recv_a[0, pair, tp] = send_a[0, pair, tp]
        return carry

    lax.fori_loop(0, 1, attend_pair, 0)
    for c in a_pair(0):
        c.start()

    for c in vu_copies:
        c.start()
    up_copy.start()
    dn_copy.start()

    dl_copy.wait()
    x_own.wait()
    x_all.wait_recv()
    partial = lax.dot_general(
        xr[...].reshape(256, 256), dl_v[...], (((1,), (1,)), ((), ())),
        preferred_element_type=F32,
    )
    ps[...] = partial.astype(BF).reshape(16, 16, WIDTH)
    p_copies = [
        copy_to(ps.at[t], pr.at[k], ss_p, rs_p, (dp, t))
        for k, t in enumerate(plane)
    ]
    for c in p_copies:
        c.start()
    p_all = all_of(pr, ss_p, rs_p, next_device)

    def attend_and_send(pair, carry):
        attend_pair(pair, carry)
        for c in a_pair(pair):
            c.start()
        return carry

    lax.fori_loop(1, 4, attend_and_send, 0)

    freq_copy.wait()
    x_copy.wait()
    x0 = x_in[...].astype(F32)
    x_scale = lax.rsqrt(jnp.mean(x0 * x0, axis=-1, keepdims=True) + EPSILON)
    p_all.wait_recv()
    comp = ps[tp].astype(F32)
    for k in range(15):
        comp = comp + pr[k].astype(F32)
    comp = comp * x_scale
    lat = comp[:, :LAT]
    lat = lat * lax.rsqrt(jnp.mean(lat * lat, axis=-1, keepdims=True) + EPSILON)
    rope = comp[:, LAT:]
    swapped = jnp.concatenate([rope[:, 32:], rope[:, :32]], axis=-1)
    row = lax.broadcasted_iota(jnp.int32, (16, 64), 0)
    position = row // 8
    for r in range(8):
        position = position + jnp.where(row % 8 == r, lens[r], 0)
    cosine, sine = cos_sin(position.astype(F32) * freq_in[...])
    first = lax.broadcasted_iota(jnp.int32, (16, 64), 1) < 32
    rotated = rope * cosine + swapped * jnp.where(first, -sine, sine)
    keys_b[:, :LAT] = lat.astype(BF)
    keys_b[:, LAT:] = rotated.astype(BF)
    keys_f[...] = lat.astype(BF).astype(F32)

    key_s[...] = jnp.concatenate([lat[:8, :256], lat[:8, 256:]], axis=0).astype(BF)
    key_r[tp] = key_s[...]
    k_copies = [
        copy_to(key_s, key_r.at[tp], ss_k, rs_k, (dp, t)) for k, t in enumerate(plane)
    ]
    for c in k_copies:
        c.start()
    k_all = all_of(key_r.at[pl.ds(0, 15)], ss_k, rs_k, next_device)

    def fresh_scores(step, r):
        fresh = jnp.dot(keys_b[...], q_v[step, r], preferred_element_type=F32).T * SCORE_SCALE
        lane = lax.broadcasted_iota(jnp.int32, (128, 16), 1)
        s0 = jnp.sum(jnp.where(lane == r, fresh, 0.0), axis=-1, keepdims=True)
        s1 = jnp.sum(jnp.where(lane == r + 8, fresh, 0.0), axis=-1, keepdims=True)
        return s0, s1

    def mix_row(r, mix):
        s0, _ = fresh_scores(0, r)
        m_old = m_v[r, :128]
        m = jnp.maximum(m_old, s0)
        cached = jnp.exp(m_old - m) * l_v[r, :128]
        p0 = jnp.exp(s0 - m)
        inverse = 1.0 / (cached + p0)
        lane = lax.broadcasted_iota(jnp.int32, (128, 128), 1)
        mix = jnp.where(lane == r, cached * inverse, mix)
        return jnp.where(lane == r + 8, p0 * inverse, mix)

    mix = lax.fori_loop(0, 8, mix_row, jnp.zeros((128, 128), F32))
    mix_s[...] = mix.reshape(16, 8, 128)
    mix_r[tp] = mix_s[tp]
    m_copies = [
        copy_to(mix_s.at[t], mix_r.at[tp], ss_m, rs_m, (dp, t))
        for k, t in enumerate(plane)
    ]
    for c in m_copies:
        c.start()
    m_all = all_of(mix_r.at[pl.ds(0, 15)], ss_m, rs_m, next_device)

    def finish_row(r):
        s0, s1 = fresh_scores(1, r)
        m_old = m_v[r, 128:]
        m = jnp.maximum(jnp.maximum(m_old, s0), s1)
        keep = jnp.exp(m_old - m)
        p0 = jnp.exp(s0 - m)
        p1 = jnp.exp(s1 - m)
        inverse = 1.0 / (keep * l_v[r, 128:] + p0 + p1)
        k0 = keys_f[pl.ds(r, 1), :]
        k1 = keys_f[pl.ds(r + 8, 1), :]
        o = o_v[r] * (keep * inverse) + (p0 * inverse) * k0 + (p1 * inverse) * k1
        return o.reshape(16, 8, LAT)

    def finish_four(g, carry):
        for j in range(2):
            pair = 2 * g + j
            both = [finish_row(2 * pair), finish_row(2 * pair + 1)]
            send_a[1, pair] = jnp.concatenate(both, axis=1).astype(BF)
            recv_a[1, pair, tp] = send_a[1, pair, tp]
        for c in a_copies(1, g):
            c.start()
        return carry

    lax.fori_loop(0, 2, finish_four, 0)

    def values(step):
        def four(g, carry):
            a_all(step, g).wait_recv()
            head = lax.broadcasted_iota(jnp.int32, (8, 128), 0)[None]
            for j in range(2):
                pair = 2 * g + j
                a = recv_a[step, pair].reshape(256, LAT)
                full = jnp.dot(a, vu_v[...], preferred_element_type=F32)
                full = full.reshape(32, 8, 1024)
                own = jnp.where(head == 0, full[:, :, :128], 0.0)
                for h in range(1, 8):
                    own = jnp.where(head == h, full[:, :, h * 128:(h + 1) * 128], own)
                for b in range(32):
                    at = pl.multiple_of((b // 2) * 64 + (2 * pair + b % 2) * 8, 8)
                    val_f[pl.ds(at, 8), :] = own[b]
            return carry

        lax.fori_loop(0, 2, four, 0)
        if step == 0:
            k_all.wait_recv()
            m_all.wait_recv()

            def spread(src, carry):
                tile = mix_r[src]
                for r in range(8):
                    at = pl.ds(pl.multiple_of(src * 64 + r * 8, 8), 8)
                    keep_f[at, :] = jnp.broadcast_to(tile[:, r:r + 1], (8, 128))
                    fresh_f[at, :] = jnp.broadcast_to(tile[:, r + 8:r + 9], (8, 128))
                return carry

            lax.fori_loop(0, 16, spread, 0)
            keys = key_r[...].astype(F32)
            keys = jnp.concatenate([keys[:, :8], keys[:, 8:]], axis=2).reshape(128, LAT).astype(BF)
            projected = jnp.dot(keys, vu_v[...], preferred_element_type=F32)
        for h in range(8):
            cols = slice(h * 128, (h + 1) * 128)
            own = pl.ds(h, 128, stride=8)
            if step == 0:
                mixed = keep_f[own, :] * val_f[own, :] + fresh_f[own, :] * projected[:, cols]
                val_b[0, :, cols] = mixed.astype(BF)
            else:
                val_b[1, :, cols] = val_f[own, :].astype(BF)

    def ways(order):
        return ((order[0:3], order[3:6]), (order[6:7], order[7:8]))

    c_cols = ways([b * 2 + c for b in (y, y_up, y_dn, y_far) for c in range(2)])
    e_cols = ways(list(range(8)))

    def fold(a):
        return jnp.concatenate([a[..., :256], a[..., 256:]], axis=-2)

    def unfold(a):
        return jnp.concatenate([a[..., :8, :], a[..., 8:, :]], axis=-1)

    class Sum:
        def __init__(self, cols, parts, sems):
            self.cols, self.parts = cols, parts
            self.ss1, self.rs1, self.ss2, self.rs2 = sems

        def share(self, step, i, way, k):
            send1 = self.parts[i][0]
            if way == 0:
                return send1.at[step, 0, :, (x + k) % 4]
            return send1.at[step, 1, (z + k) % 4]

        def first(self, step, i, way, n):
            on = on_x if way == 0 else on_z
            k = LINE[n]
            return copy_to(self.share(step, i, way, k), self.parts[i][1].at[step, way, n],
                           self.ss1.at[step, i, way], self.rs1.at[step, i, way], on[k])

        def last(self, step, i, way, n):
            on, here = (on_z, z) if way == 0 else (on_x, x)
            k = LINE[n]
            return copy_to(self.parts[i][2].at[step, way, (here + k) % 4], self.parts[i][3].at[step, way, n],
                           self.ss2.at[step, i, way], self.rs2.at[step, i, way], on[k])

        def first_all(self, step, i, way):
            return all_of(self.parts[i][1].at[step, way], self.ss1.at[step, i, way],
                          self.rs1.at[step, i, way], next_device)

        def last_all(self, step, i, way):
            return all_of(self.parts[i][3].at[step, way], self.ss2.at[step, i, way],
                          self.rs2.at[step, i, way], next_device)

        def begin(self, step, i, multiply):
            for way in range(2):
                for m, col in enumerate(self.cols[i][way]):
                    block = fold(multiply(col).reshape(16, 8, 512)).astype(BF)
                    self.parts[i][0][step, way, :, :, :, m * 256:(m + 1) * 256] = block.reshape(4, 4, 16, 256)
                for n in range(3):
                    self.first(step, i, way, n).start()

        def middle(self, step, i):
            for way in range(2):
                self.first_all(step, i, way).wait_recv()
                total = self.share(step, i, way, 0)[...].astype(F32)
                for n in range(3):
                    total = total + self.parts[i][1][step, way, n].astype(F32)
                self.parts[i][2][step, way] = total.astype(BF)
                for n in range(3):
                    self.last(step, i, way, n).start()

        def end(self, step, i, way):
            self.last_all(step, i, way).wait_recv()
            total = self.parts[i][2][step, way, z if way == 0 else x].astype(F32)
            for n in range(3):
                total = total + self.parts[i][3][step, way, n].astype(F32)
            return total

        def drain(self):
            for step in range(2):
                for i in range(2):
                    for way in range(2):
                        self.first_all(step, i, way).wait_send()
                        self.last_all(step, i, way).wait_send()

    c_sum = Sum(
        c_cols,
        ((c_send1, c_recv1, c_send2, c_recv2), (c_tail1, c_tail2, c_tail3, c_tail4)),
        (ss_c1, rs_c1, ss_c2, rs_c2),
    )
    e_sum = Sum(
        e_cols,
        ((e_send1, e_recv1, e_send2, e_recv2), (e_tail1, e_tail2, e_tail3, e_tail4)),
        (ss_e1, rs_e1, ss_e2, rs_e2),
    )

    def begin_c(step, i):
        c_sum.begin(step, i, lambda col: jnp.dot(
            val_b[step], w_v[col], preferred_element_type=F32
        ))

    rows_in = (gath, gath_tail)

    def g_first(step, i, way, n):
        on = on_x if way == 0 else on_z
        block = rows_in[i].at[step, way, z, x]
        return copy_to(block, block, ss_g.at[step, i, way, 0], rs_g.at[step, i, way, 0], on[LINE[n]])

    def g_last(step, i, way, n):
        on = on_z if way == 0 else on_x
        block = rows_in[i].at[step, 0, z] if way == 0 else rows_in[i].at[step, 1, :, x]
        return copy_to(block, block, ss_g.at[step, i, way, 1], rs_g.at[step, i, way, 1], on[LINE[n]])

    def g_first_all(step, i, way):
        return all_of(rows_in[i].at[step, way, 0, pl.ds(0, 3)],
                      ss_g.at[step, i, way, 0], rs_g.at[step, i, way, 0], next_device)

    def g_last_all(step, i, way):
        return all_of(rows_in[i].at[step, way, pl.ds(0, 3)],
                      ss_g.at[step, i, way, 1], rs_g.at[step, i, way, 1], next_device)

    def hidden(step, i):
        for way in range(2):
            total = c_sum.end(step, i, way)
            for m, col in enumerate(c_cols[i][way]):
                own = x_in[:, pl.ds(pl.multiple_of(col * 512, 512), 512)].astype(F32)[step * 8:step * 8 + 8]
                here = slice(m * 256, (m + 1) * 256)
                block = total[:, here] + fold(own)
                hid[step, col] = block
                rows_in[i][step, way, z, x, :, here] = block.astype(BF)
            for n in range(3):
                g_first(step, i, way, n).start()

    def gather(step, i):
        for way in range(2):
            g_first_all(step, i, way).wait_recv()
            for n in range(3):
                g_last(step, i, way, n).start()

    def expand(step, i):
        total = None
        squares = None
        for way in range(2):
            g_last_all(step, i, way).wait_recv()
            for m, col in enumerate(c_cols[i][way]):
                rows = rows_in[i][step, way, :, :, :, m * 256:(m + 1) * 256].reshape(16, 16, 256)
                a = unfold(rows.astype(F32)).reshape(128, 512)
                more = jnp.sum(a * a, axis=-1, keepdims=True)
                term = jnp.dot(a.astype(BF), up_v[col], preferred_element_type=F32)
                total = term if total is None else total + term
                squares = more if squares is None else squares + more
        if i == 0:
            acc[step] = total
            square[step] = squares
        else:
            v = (acc[step] + total) * lax.rsqrt((square[step] + squares) / D + EPSILON)
            act[step] = (v / (1.0 + jnp.exp(-v))).astype(BF)

    def begin_e(step, i):
        e_sum.begin(step, i, lambda col: jnp.dot(
            act[step], dn_v[:, col * 512:(col + 1) * 512], preferred_element_type=F32
        ))

    def finish(step, i):
        for way in range(2):
            total = e_sum.end(step, i, way)
            for m, col in enumerate(e_cols[i][way]):
                result = unfold(hid[step, col] + total[:, m * 256:(m + 1) * 256])
                out[step, :, col * 512:(col + 1) * 512] = result.astype(BF)

    def weights_near():
        w_up[1].wait_recv()
        w_sib_dn[1].start()
        w_dn[1].wait_recv()
        w_sib_up[1].start()
        ow_copy.wait()
        w_sib.wait_recv()
        for c in w_sib_up + w_sib_dn:
            c.wait_recv()

    def weights_far():
        w_up2.wait_recv()
        w_dn2.wait_recv()
        w_sib_far.start()
        w_sib_far.wait_recv()

    w_up[0].wait_recv()
    w_up2.start()
    w_sib_dn[0].start()
    w_dn[0].wait_recv()
    w_dn2.start()
    w_sib_up[0].start()
    for c in vu_copies:
        c.wait()
    values(0)
    weights_near()
    begin_c(0, 0)
    values(1)
    begin_c(1, 0)
    c_sum.middle(0, 0)
    weights_far()
    begin_c(0, 1)
    begin_c(1, 1)
    c_sum.middle(1, 0)
    hidden(0, 0)
    c_sum.middle(0, 1)
    c_sum.middle(1, 1)
    hidden(1, 0)
    hidden(0, 1)
    gather(0, 0)
    gather(0, 1)
    hidden(1, 1)
    gather(1, 0)
    up_copy.wait()
    expand(0, 0)
    gather(1, 1)
    expand(0, 1)
    dn_copy.wait()
    begin_e(0, 0)
    expand(1, 0)
    begin_e(0, 1)
    expand(1, 1)
    begin_e(1, 0)
    begin_e(1, 1)
    e_sum.middle(0, 0)
    e_sum.middle(0, 1)
    e_sum.middle(1, 0)
    e_sum.middle(1, 1)
    finish(0, 0)
    finish(0, 1)
    finish(1, 0)
    finish(1, 1)

    for c in (x_all, p_all, k_all, m_all):
        c.wait_send()

    def drain(i, carry):
        a_all(i // 2, i % 2).wait_send()
        return carry

    lax.fori_loop(0, 4, drain, 0)
    for c in w_up + w_dn + w_sib_dn + w_sib_up + [w_sib, w_up2, w_dn2, w_sib_far]:
        c.wait_send()
    c_sum.drain()
    e_sum.drain()
    for step in range(2):
        for i in range(2):
            for way in range(2):
                g_first_all(step, i, way).wait_send()
                g_last_all(step, i, way).wait_send()


def layer(lengths, inputs, frequency, queries, cache, down_latent, value_up, output_weight, up_weight, down_weight):
    vmem, hbm = pl.BlockSpec(memory_space=pltpu.VMEM), pl.BlockSpec(memory_space=pl.ANY)
    dma = pltpu.SemaphoreType.DMA
    scratch = [
        pltpu.VMEM((16, D), BF),
        pltpu.VMEM((16, 64), F32),
        pltpu.VMEM((2, 8, WIDTH, 128), BF),
        pltpu.VMEM((8, WIDTH, CTX), BF),
        pltpu.VMEM((WIDTH, 256), BF),
        pltpu.VMEM((LAT, 1024), BF),
        pltpu.VMEM((8, 1024, 512), BF),
        pltpu.VMEM((8, 512, FF), BF),
        pltpu.VMEM((FF, D), BF),
        pltpu.VMEM((16, 16, 256), BF),
        pltpu.VMEM((16, 16, WIDTH), BF),
        pltpu.VMEM((15, 16, WIDTH), BF),
        pltpu.VMEM((16, WIDTH), BF),
        pltpu.VMEM((16, LAT), F32),
        pltpu.VMEM((8, 128, LAT), F32),
        pltpu.VMEM((8, 256, 1), F32),
        pltpu.VMEM((8, 256, 1), F32),
        pltpu.VMEM((2, 4, 16, 16, LAT), BF),
        pltpu.VMEM((2, 4, 16, 16, LAT), BF),
        pltpu.VMEM((1024, 128), F32),
        pltpu.VMEM((2, 128, 1024), BF),
        pltpu.VMEM((2, 8, 16, 256), F32),
        pltpu.VMEM((2, 128, FF), F32),
        pltpu.VMEM((2, 128, 1), F32),
        pltpu.VMEM((2, 128, FF), BF),
    ]
    scratch += [
        pltpu.VMEM((16, 8, 128), F32),
        pltpu.VMEM((16, 8, 128), F32),
        pltpu.VMEM((16, 256), BF),
        pltpu.VMEM((16, 16, 256), BF),
        pltpu.VMEM((1024, 128), F32),
        pltpu.VMEM((1024, 128), F32),
    ]
    for gathers in (1, 0):
        for width in (768, 256):
            scratch += [
                pltpu.VMEM((2, 2, 4, 4, 16, width), BF),
                pltpu.VMEM((2, 2, 3, 4, 16, width), BF),
                pltpu.VMEM((2, 2, 4, 16, width), BF),
                pltpu.VMEM((2, 2, 3, 16, width), BF),
            ] + [pltpu.VMEM((2, 2, 4, 4, 16, width), BF)] * gathers
    scratch += [dma((8,)), dma((8,)), dma((7,)), dma((8,))]
    scratch += [dma] * 4 + [dma((2, 2))] * 2 + [dma] * 4 + [dma((12,))] * 2 + [dma((2, 2, 2, 2))] * 2
    scratch += [dma((2, 2, 2))] * 8
    return pl.pallas_call(
        kernel,
        out_shape=jax.ShapeDtypeStruct((2, 8, D), BF),
        in_specs=[pl.BlockSpec(memory_space=pltpu.SMEM)] + [hbm] * 9,
        out_specs=vmem,
        scratch_shapes=scratch,
        compiler_params=pltpu.CompilerParams(
            collective_id=0, has_side_effects=True, vmem_limit_bytes=60 * 1024 * 1024
        ),
    )(lengths, inputs, frequency, queries, cache, down_latent, value_up, output_weight, up_weight, down_weight)


def body(queries, latent_cache, lengths, inputs, down_latent, value_up, output_weight, up_weight, down_weight):
    half = ROPE_BASE ** (-np.arange(32, dtype=np.float32) / np.float32(32))
    frequency = np.tile(half.astype(np.float32), (16, 2))
    return layer(
        lengths, inputs.reshape(16, D), jnp.asarray(frequency),
        jnp.swapaxes(queries, 2, 3), jnp.swapaxes(latent_cache, 1, 2), down_latent.T,
        value_up, output_weight, up_weight.reshape(8, 512, FF), down_weight,
    )


def solution(mesh):
    return jax.shard_map(
        body,
        mesh=mesh,
        in_specs=(
            P(None, ("dp", "tp"), None, None),
            P(("dp", "tp"), None, None),
            P(("dp", "tp")),
            P(None, ("dp", "tp"), None),
            P("tp", None),
            P("tp", None, None),
            P("tp", "dp"),
            P(None, "tp"),
            P("tp", None),
        ),
        out_specs=P(None, ("dp", "tp"), None),
        check_vma=False,
    )
```

```python
import math

import jax
import jax.numpy as jnp
import numpy as np
from jax import lax
from jax.experimental import pallas as pl
from jax.experimental.pallas import tpu as pltpu
from jax.sharding import PartitionSpec as P

LAT = 512
WIDTH = 576
CTX = 512
D = 4096
FF = 640
EPSILON = 1e-06
SCORE_SCALE = 192.0 ** (-0.5)
ROPE_BASE = 10000.0
NEG = -1e30
BF = jnp.bfloat16
F32 = jnp.float32
MESH = pl.DeviceIdType.MESH

PLANE = (
    (0, 1), (0, 3), (1, 0), (3, 0), (2, 1), (1, 2), (2, 3), (3, 2),
    (2, 2), (1, 1), (3, 3), (1, 3), (3, 1), (0, 2), (2, 0),
)
LINE = (1, 3, 2)


def copy_to(src, dst, send_sem, recv_sem, device):
    return pltpu.make_async_remote_copy(
        src_ref=src, dst_ref=dst, send_sem=send_sem, recv_sem=recv_sem,
        device_id=device, device_id_type=MESH,
    )


def all_of(region, send_sem, recv_sem, device):
    return copy_to(region, region, send_sem, recv_sem, device)


def cos_sin(angles):
    turns = jnp.floor(angles * (0.5 / np.pi) + 0.5)
    rest = angles - turns * 6.28125
    rest = rest - turns * (2 * np.pi - 6.28125)
    square = rest * rest
    cosine = jnp.zeros_like(square)
    sine = jnp.zeros_like(square)
    for n in range(8, -1, -1):
        cosine = cosine * square + (-1.0) ** n / math.factorial(2 * n)
        sine = sine * square + (-1.0) ** n / math.factorial(2 * n + 1)
    return cosine, sine * rest


def kernel(
    lens, x_hbm, freq_hbm, q_hbm, c_hbm, dl_hbm, vu_hbm, ow_hbm, up_hbm, dn_hbm,
    out,
    x_in, freq_in, q_v, c_v, dl_v, vu_v, w_v, up_v, dn_v,
    xr, ps, pr, keys_b, keys_f, o_v, m_v, l_v,
    send_a, recv_a, val_f, val_b, hid, acc, square, act,
    mix_s, mix_r, key_s, key_r, keep_f, fresh_f,
    c_send1, c_recv1, c_send2, c_recv2, gath, c_tail1, c_tail2, c_tail3, c_tail4, gath_tail,
    e_send1, e_recv1, e_send2, e_recv2, e_tail1, e_tail2, e_tail3, e_tail4,
    sem_q, sem_c, sem_w, sem_vu,
    ss_x, rs_x, ss_p, rs_p, ss_a, rs_a, ss_m, rs_m, ss_k, rs_k, ss_w, rs_w, ss_g, rs_g,
    ss_c1, rs_c1, ss_c2, rs_c2, ss_e1, rs_e1, ss_e2, rs_e2,
):
    dp = lax.axis_index("dp")
    tp = lax.axis_index("tp")
    y, core = dp // 2, dp % 2
    z, x = tp // 4, tp % 4
    plane = [((z + dz) % 4) * 4 + (x + dx) % 4 for dz, dx in PLANE]
    on_x = {k: (dp, z * 4 + (x + k) % 4) for k in LINE}
    on_z = {k: (dp, ((z + k) % 4) * 4 + x) for k in LINE}
    next_device = (dp, plane[0])
    y_up, y_dn, y_far = (y + 1) % 4, (y + 3) % 4, (y + 2) % 4
    sibling = y * 2 + 1 - core

    barrier = pltpu.get_barrier_semaphore()
    partners = [(dp, t) for t in plane] + [
        (sibling, tp), (y_up * 2 + core, tp), (y_dn * 2 + core, tp)
    ]
    for device in partners:
        pl.semaphore_signal(barrier, inc=1, device_id=device, device_id_type=MESH)

    def q_copy(r):
        return pltpu.make_async_copy(q_hbm.at[:, r], q_v.at[:, r], sem_q.at[r])

    def c_copy(r):
        return pltpu.make_async_copy(c_hbm.at[r], c_v.at[r], sem_c.at[r])

    dl_copy = pltpu.make_async_copy(dl_hbm, dl_v, sem_w.at[0])
    ow_copy = pltpu.make_async_copy(ow_hbm, w_v.at[dp], sem_w.at[1])
    up_copy = pltpu.make_async_copy(up_hbm, up_v, sem_w.at[2])
    dn_copy = pltpu.make_async_copy(dn_hbm, dn_v, sem_w.at[3])
    x_copy = pltpu.make_async_copy(x_hbm, x_in, sem_w.at[4])
    freq_copy = pltpu.make_async_copy(freq_hbm, freq_in, sem_w.at[5])
    vu_copies = [
        pltpu.make_async_copy(vu_hbm.at[h], vu_v.at[:, pl.ds(h * 128, 128)], sem_vu.at[h])
        for h in range(8)
    ]
    x_copy.start()
    for r in range(2):
        q_copy(r).start()
        c_copy(r).start()
    dl_copy.start()

    pl.semaphore_wait(barrier, len(partners))

    def x_slice(t):
        return x_hbm.at[:, pl.ds(pl.multiple_of(t * 256, 256), 256)]

    x_copies = [
        copy_to(x_slice(t), xr.at[tp], ss_x, rs_x, (dp, t))
        for k, t in enumerate(plane)
    ]
    for c in x_copies:
        c.start()
    x_all = all_of(xr.at[pl.ds(0, 15)], ss_x, rs_x, next_device)
    for r in range(2, 8):
        q_copy(r).start()
        c_copy(r).start()
    freq_copy.start()
    x_own = pltpu.make_async_copy(x_slice(tp), xr.at[tp], sem_w.at[6])
    x_own.start()

    lo, hi = pl.ds(0, 512), pl.ds(512, 512)
    up_dev, dn_dev, sib_dev = (y_up * 2 + core, tp), (y_dn * 2 + core, tp), (sibling, tp)
    w_up = [
        copy_to(ow_hbm.at[s], w_v.at[dp, s], ss_w.at[i], rs_w.at[i], up_dev)
        for i, s in enumerate((lo, hi))
    ]
    w_dn = [
        copy_to(ow_hbm.at[s], w_v.at[dp, s], ss_w.at[2 + i], rs_w.at[2 + i], dn_dev)
        for i, s in enumerate((hi, lo))
    ]
    w_sib = copy_to(ow_hbm, w_v.at[dp], ss_w.at[4], rs_w.at[4], sib_dev)
    from_dn, from_up, from_far = y_dn * 2 + core, y_up * 2 + core, y_far * 2 + core
    w_up2 = copy_to(w_v.at[from_dn, lo], w_v.at[from_dn, lo], ss_w.at[5], rs_w.at[5], up_dev)
    w_dn2 = copy_to(w_v.at[from_up, hi], w_v.at[from_up, hi], ss_w.at[6], rs_w.at[6], dn_dev)
    w_sib_dn = [
        copy_to(w_v.at[from_dn, s], w_v.at[from_dn, s], ss_w.at[7 + i], rs_w.at[7 + i], sib_dev)
        for i, s in enumerate((lo, hi))
    ]
    w_sib_up = [
        copy_to(w_v.at[from_up, s], w_v.at[from_up, s], ss_w.at[10 + i], rs_w.at[10 + i], sib_dev)
        for i, s in enumerate((hi, lo))
    ]
    w_sib_far = copy_to(w_v.at[from_far], w_v.at[from_far], ss_w.at[9], rs_w.at[9], sib_dev)
    for c in (w_up[0], w_dn[0], w_up[1], w_dn[1], w_sib):
        c.start()
    ow_copy.start()

    def a_copies(step, g):
        rows = pl.ds(2 * g, 2)
        return [
            copy_to(send_a.at[step, rows, t], recv_a.at[step, rows, tp],
                    ss_a.at[step, g], rs_a.at[step, g], (dp, t))
            for t in plane
        ]

    def a_pair(pair):
        return [
            copy_to(send_a.at[0, pair, t], recv_a.at[0, pair, tp],
                    ss_a.at[0, pair // 2], rs_a.at[0, pair // 2], (dp, t))
            for t in plane
        ]

    def a_all(step, g):
        return all_of(recv_a.at[step, pl.ds(2 * g, 2), pl.ds(0, 15)],
                      ss_a.at[step, g], rs_a.at[step, g], next_device)

    def attend_row(r):
        q_copy(r).wait()
        c_copy(r).wait()
        q = jnp.concatenate([q_v[0, r], q_v[1, r]], axis=1)
        k = c_v[r]
        s = lax.dot_general(
            q, k, (((0,), (0,)), ((), ())), preferred_element_type=F32
        ) * SCORE_SCALE
        position = lax.broadcasted_iota(jnp.int32, (1, CTX), 1)
        s = jnp.where(position < lens[r], s, NEG)
        m = jnp.max(s, axis=-1, keepdims=True)
        p = jnp.exp(s - m)
        total = jnp.sum(p, axis=-1, keepdims=True)
        l_v[r] = total
        m_v[r] = m
        o = lax.dot_general(
            p.astype(BF), k[:LAT], (((1,), (1,)), ((), ())), preferred_element_type=F32
        )
        o_v[r] = o[128:]
        return (o[:128] * (1.0 / total[:128])).reshape(16, 8, LAT)

    def attend_pair(pair, carry):
        both = [attend_row(2 * pair), attend_row(2 * pair + 1)]
        send_a[0, pair] = jnp.concatenate(both, axis=1).astype(BF)
        recv_a[0, pair, tp] = send_a[0, pair, tp]
        return carry

    lax.fori_loop(0, 1, attend_pair, 0)
    for c in a_pair(0):
        c.start()

    for c in vu_copies:
        c.start()
    up_copy.start()
    dn_copy.start()

    dl_copy.wait()
    x_own.wait()
    x_all.wait_recv()
    partial = lax.dot_general(
        xr[...].reshape(256, 256), dl_v[...], (((1,), (1,)), ((), ())),
        preferred_element_type=F32,
    )
    ps[...] = partial.astype(BF).reshape(16, 16, WIDTH)
    p_copies = [
        copy_to(ps.at[t], pr.at[k], ss_p, rs_p, (dp, t))
        for k, t in enumerate(plane)
    ]
    for c in p_copies:
        c.start()
    p_all = all_of(pr, ss_p, rs_p, next_device)

    def attend_and_send(pair, carry):
        attend_pair(pair, carry)
        for c in a_pair(pair):
            c.start()
        return carry

    lax.fori_loop(1, 4, attend_and_send, 0)

    freq_copy.wait()
    x_copy.wait()
    x0 = x_in[...].astype(F32)
    x_scale = lax.rsqrt(jnp.mean(x0 * x0, axis=-1, keepdims=True) + EPSILON)
    p_all.wait_recv()
    comp = ps[tp].astype(F32)
    for k in range(15):
        comp = comp + pr[k].astype(F32)
    comp = comp * x_scale
    lat = comp[:, :LAT]
    lat = lat * lax.rsqrt(jnp.mean(lat * lat, axis=-1, keepdims=True) + EPSILON)
    rope = comp[:, LAT:]
    swapped = jnp.concatenate([rope[:, 32:], rope[:, :32]], axis=-1)
    row = lax.broadcasted_iota(jnp.int32, (16, 64), 0)
    position = row // 8
    for r in range(8):
        position = position + jnp.where(row % 8 == r, lens[r], 0)
    cosine, sine = cos_sin(position.astype(F32) * freq_in[...])
    first = lax.broadcasted_iota(jnp.int32, (16, 64), 1) < 32
    rotated = rope * cosine + swapped * jnp.where(first, -sine, sine)
    keys_b[:, :LAT] = lat.astype(BF)
    keys_b[:, LAT:] = rotated.astype(BF)
    keys_f[...] = lat.astype(BF).astype(F32)

    key_s[...] = jnp.concatenate([lat[:8, :256], lat[:8, 256:]], axis=0).astype(BF)
    key_r[tp] = key_s[...]
    k_copies = [
        copy_to(key_s, key_r.at[tp], ss_k, rs_k, (dp, t)) for k, t in enumerate(plane)
    ]
    for c in k_copies:
        c.start()
    k_all = all_of(key_r.at[pl.ds(0, 15)], ss_k, rs_k, next_device)

    def fresh_scores(step, r):
        fresh = jnp.dot(keys_b[...], q_v[step, r], preferred_element_type=F32).T * SCORE_SCALE
        lane = lax.broadcasted_iota(jnp.int32, (128, 16), 1)
        s0 = jnp.sum(jnp.where(lane == r, fresh, 0.0), axis=-1, keepdims=True)
        s1 = jnp.sum(jnp.where(lane == r + 8, fresh, 0.0), axis=-1, keepdims=True)
        return s0, s1

    def mix_row(r, mix):
        s0, _ = fresh_scores(0, r)
        m_old = m_v[r, :128]
        m = jnp.maximum(m_old, s0)
        cached = jnp.exp(m_old - m) * l_v[r, :128]
        p0 = jnp.exp(s0 - m)
        inverse = 1.0 / (cached + p0)
        lane = lax.broadcasted_iota(jnp.int32, (128, 128), 1)
        mix = jnp.where(lane == r, cached * inverse, mix)
        return jnp.where(lane == r + 8, p0 * inverse, mix)

    mix = lax.fori_loop(0, 8, mix_row, jnp.zeros((128, 128), F32), unroll=True)
    mix_s[...] = mix.reshape(16, 8, 128)
    mix_r[tp] = mix_s[tp]
    m_copies = [
        copy_to(mix_s.at[t], mix_r.at[tp], ss_m, rs_m, (dp, t))
        for k, t in enumerate(plane)
    ]
    for c in m_copies:
        c.start()
    m_all = all_of(mix_r.at[pl.ds(0, 15)], ss_m, rs_m, next_device)

    def finish_row(r):
        s0, s1 = fresh_scores(1, r)
        m_old = m_v[r, 128:]
        m = jnp.maximum(jnp.maximum(m_old, s0), s1)
        keep = jnp.exp(m_old - m)
        p0 = jnp.exp(s0 - m)
        p1 = jnp.exp(s1 - m)
        inverse = 1.0 / (keep * l_v[r, 128:] + p0 + p1)
        k0 = keys_f[pl.ds(r, 1), :]
        k1 = keys_f[pl.ds(r + 8, 1), :]
        o = o_v[r] * (keep * inverse) + (p0 * inverse) * k0 + (p1 * inverse) * k1
        return o.reshape(16, 8, LAT)

    def finish_four(g, carry):
        for j in range(2):
            pair = 2 * g + j
            both = [finish_row(2 * pair), finish_row(2 * pair + 1)]
            send_a[1, pair] = jnp.concatenate(both, axis=1).astype(BF)
            recv_a[1, pair, tp] = send_a[1, pair, tp]
        for c in a_copies(1, g):
            c.start()
        return carry

    lax.fori_loop(0, 2, finish_four, 0)

    def values(step):
        def four(g, carry):
            a_all(step, g).wait_recv()
            head = lax.broadcasted_iota(jnp.int32, (8, 128), 0)[None]
            for j in range(2):
                pair = 2 * g + j
                a = recv_a[step, pair].reshape(256, LAT)
                full = jnp.dot(a, vu_v[...], preferred_element_type=F32)
                full = full.reshape(32, 8, 1024)
                own = jnp.where(head == 0, full[:, :, :128], 0.0)
                for h in range(1, 8):
                    own = jnp.where(head == h, full[:, :, h * 128:(h + 1) * 128], own)
                for b in range(32):
                    at = pl.multiple_of((b // 2) * 64 + (2 * pair + b % 2) * 8, 8)
                    val_f[pl.ds(at, 8), :] = own[b]
            return carry

        lax.fori_loop(0, 2, four, 0)
        if step == 0:
            k_all.wait_recv()
            m_all.wait_recv()

            def spread(src, carry):
                tile = mix_r[src]
                for r in range(8):
                    at = pl.ds(pl.multiple_of(src * 64 + r * 8, 8), 8)
                    keep_f[at, :] = jnp.broadcast_to(tile[:, r:r + 1], (8, 128))
                    fresh_f[at, :] = jnp.broadcast_to(tile[:, r + 8:r + 9], (8, 128))
                return carry

            lax.fori_loop(0, 16, spread, 0)
            keys = key_r[...].astype(F32)
            keys = jnp.concatenate([keys[:, :8], keys[:, 8:]], axis=2).reshape(128, LAT).astype(BF)
            projected = jnp.dot(keys, vu_v[...], preferred_element_type=F32)
        for h in range(8):
            cols = slice(h * 128, (h + 1) * 128)
            own = pl.ds(h, 128, stride=8)
            if step == 0:
                mixed = keep_f[own, :] * val_f[own, :] + fresh_f[own, :] * projected[:, cols]
                val_b[0, :, cols] = mixed.astype(BF)
            else:
                val_b[1, :, cols] = val_f[own, :].astype(BF)

    def ways(order):
        return ((order[0:3], order[3:6]), (order[6:7], order[7:8]))

    c_cols = ways([b * 2 + c for b in (y, y_up, y_dn, y_far) for c in range(2)])
    e_cols = ways(list(range(8)))

    def fold(a):
        return jnp.concatenate([a[..., :256], a[..., 256:]], axis=-2)

    def unfold(a):
        return jnp.concatenate([a[..., :8, :], a[..., 8:, :]], axis=-1)

    class Sum:
        def __init__(self, cols, parts, sems):
            self.cols, self.parts = cols, parts
            self.ss1, self.rs1, self.ss2, self.rs2 = sems

        def share(self, step, i, way, k):
            send1 = self.parts[i][0]
            if way == 0:
                return send1.at[step, 0, :, (x + k) % 4]
            return send1.at[step, 1, (z + k) % 4]

        def first(self, step, i, way, n):
            on = on_x if way == 0 else on_z
            k = LINE[n]
            return copy_to(self.share(step, i, way, k), self.parts[i][1].at[step, way, n],
                           self.ss1.at[step, i, way], self.rs1.at[step, i, way], on[k])

        def last(self, step, i, way, n):
            on, here = (on_z, z) if way == 0 else (on_x, x)
            k = LINE[n]
            return copy_to(self.parts[i][2].at[step, way, (here + k) % 4], self.parts[i][3].at[step, way, n],
                           self.ss2.at[step, i, way], self.rs2.at[step, i, way], on[k])

        def first_all(self, step, i, way):
            return all_of(self.parts[i][1].at[step, way], self.ss1.at[step, i, way],
                          self.rs1.at[step, i, way], next_device)

        def last_all(self, step, i, way):
            return all_of(self.parts[i][3].at[step, way], self.ss2.at[step, i, way],
                          self.rs2.at[step, i, way], next_device)

        def begin(self, step, i, multiply):
            for way in range(2):
                for m, col in enumerate(self.cols[i][way]):
                    block = fold(multiply(col).reshape(16, 8, 512)).astype(BF)
                    self.parts[i][0][step, way, :, :, :, m * 256:(m + 1) * 256] = block.reshape(4, 4, 16, 256)
                for n in range(3):
                    self.first(step, i, way, n).start()

        def middle(self, step, i):
            for way in range(2):
                self.first_all(step, i, way).wait_recv()
                total = self.share(step, i, way, 0)[...].astype(F32)
                for n in range(3):
                    total = total + self.parts[i][1][step, way, n].astype(F32)
                self.parts[i][2][step, way] = total.astype(BF)
                for n in range(3):
                    self.last(step, i, way, n).start()

        def end(self, step, i, way):
            self.last_all(step, i, way).wait_recv()
            total = self.parts[i][2][step, way, z if way == 0 else x].astype(F32)
            for n in range(3):
                total = total + self.parts[i][3][step, way, n].astype(F32)
            return total

        def drain(self):
            for step in range(2):
                for i in range(2):
                    for way in range(2):
                        self.first_all(step, i, way).wait_send()
                        self.last_all(step, i, way).wait_send()

    c_sum = Sum(
        c_cols,
        ((c_send1, c_recv1, c_send2, c_recv2), (c_tail1, c_tail2, c_tail3, c_tail4)),
        (ss_c1, rs_c1, ss_c2, rs_c2),
    )
    e_sum = Sum(
        e_cols,
        ((e_send1, e_recv1, e_send2, e_recv2), (e_tail1, e_tail2, e_tail3, e_tail4)),
        (ss_e1, rs_e1, ss_e2, rs_e2),
    )

    def begin_c(step, i):
        c_sum.begin(step, i, lambda col: jnp.dot(
            val_b[step], w_v[col], preferred_element_type=F32
        ))

    rows_in = (gath, gath_tail)

    def g_first(step, i, way, n):
        on = on_x if way == 0 else on_z
        block = rows_in[i].at[step, way, z, x]
        return copy_to(block, block, ss_g.at[step, i, way, 0], rs_g.at[step, i, way, 0], on[LINE[n]])

    def g_last(step, i, way, n):
        on = on_z if way == 0 else on_x
        block = rows_in[i].at[step, 0, z] if way == 0 else rows_in[i].at[step, 1, :, x]
        return copy_to(block, block, ss_g.at[step, i, way, 1], rs_g.at[step, i, way, 1], on[LINE[n]])

    def g_first_all(step, i, way):
        return all_of(rows_in[i].at[step, way, 0, pl.ds(0, 3)],
                      ss_g.at[step, i, way, 0], rs_g.at[step, i, way, 0], next_device)

    def g_last_all(step, i, way):
        return all_of(rows_in[i].at[step, way, pl.ds(0, 3)],
                      ss_g.at[step, i, way, 1], rs_g.at[step, i, way, 1], next_device)

    def hidden(step, i):
        for way in range(2):
            total = c_sum.end(step, i, way)
            for m, col in enumerate(c_cols[i][way]):
                own = x_in[:, pl.ds(pl.multiple_of(col * 512, 512), 512)].astype(F32)[step * 8:step * 8 + 8]
                here = slice(m * 256, (m + 1) * 256)
                block = total[:, here] + fold(own)
                hid[step, col] = block
                rows_in[i][step, way, z, x, :, here] = block.astype(BF)
            for n in range(3):
                g_first(step, i, way, n).start()

    def gather(step, i):
        for way in range(2):
            g_first_all(step, i, way).wait_recv()
            for n in range(3):
                g_last(step, i, way, n).start()

    def expand(step, i):
        total = None
        squares = None
        for way in range(2):
            g_last_all(step, i, way).wait_recv()
            for m, col in enumerate(c_cols[i][way]):
                rows = rows_in[i][step, way, :, :, :, m * 256:(m + 1) * 256].reshape(16, 16, 256)
                a = unfold(rows.astype(F32)).reshape(128, 512)
                more = jnp.sum(a * a, axis=-1, keepdims=True)
                term = jnp.dot(a.astype(BF), up_v[col], preferred_element_type=F32)
                total = term if total is None else total + term
                squares = more if squares is None else squares + more
        if i == 0:
            acc[step] = total
            square[step] = squares
        else:
            v = (acc[step] + total) * lax.rsqrt((square[step] + squares) / D + EPSILON)
            act[step] = (v / (1.0 + jnp.exp(-v))).astype(BF)

    def begin_e(step, i):
        e_sum.begin(step, i, lambda col: jnp.dot(
            act[step], dn_v[:, col * 512:(col + 1) * 512], preferred_element_type=F32
        ))

    def finish(step, i):
        for way in range(2):
            total = e_sum.end(step, i, way)
            for m, col in enumerate(e_cols[i][way]):
                result = unfold(hid[step, col] + total[:, m * 256:(m + 1) * 256])
                out[step, :, col * 512:(col + 1) * 512] = result.astype(BF)

    def weights_near():
        w_up[1].wait_recv()
        w_sib_dn[1].start()
        w_dn[1].wait_recv()
        w_sib_up[1].start()
        ow_copy.wait()
        w_sib.wait_recv()
        for c in w_sib_up + w_sib_dn:
            c.wait_recv()

    def weights_far():
        w_up2.wait_recv()
        w_dn2.wait_recv()
        w_sib_far.start()
        w_sib_far.wait_recv()

    w_up[0].wait_recv()
    w_up2.start()
    w_sib_dn[0].start()
    w_dn[0].wait_recv()
    w_dn2.start()
    w_sib_up[0].start()
    for c in vu_copies:
        c.wait()
    values(0)
    weights_near()
    begin_c(0, 0)
    values(1)
    begin_c(1, 0)
    c_sum.middle(0, 0)
    weights_far()
    begin_c(0, 1)
    begin_c(1, 1)
    c_sum.middle(1, 0)
    hidden(0, 0)
    c_sum.middle(0, 1)
    c_sum.middle(1, 1)
    hidden(1, 0)
    hidden(0, 1)
    gather(0, 0)
    gather(0, 1)
    hidden(1, 1)
    gather(1, 0)
    up_copy.wait()
    expand(0, 0)
    gather(1, 1)
    expand(0, 1)
    dn_copy.wait()
    begin_e(0, 0)
    expand(1, 0)
    begin_e(0, 1)
    expand(1, 1)
    begin_e(1, 0)
    begin_e(1, 1)
    e_sum.middle(0, 0)
    e_sum.middle(0, 1)
    e_sum.middle(1, 0)
    e_sum.middle(1, 1)
    finish(0, 0)
    finish(0, 1)
    finish(1, 0)
    finish(1, 1)

    for c in (x_all, p_all, k_all, m_all):
        c.wait_send()

    def drain(i, carry):
        a_all(i // 2, i % 2).wait_send()
        return carry

    lax.fori_loop(0, 4, drain, 0)
    for c in w_up + w_dn + w_sib_dn + w_sib_up + [w_sib, w_up2, w_dn2, w_sib_far]:
        c.wait_send()
    c_sum.drain()
    e_sum.drain()
    for step in range(2):
        for i in range(2):
            for way in range(2):
                g_first_all(step, i, way).wait_send()
                g_last_all(step, i, way).wait_send()


def layer(lengths, inputs, frequency, queries, cache, down_latent, value_up, output_weight, up_weight, down_weight):
    vmem, hbm = pl.BlockSpec(memory_space=pltpu.VMEM), pl.BlockSpec(memory_space=pl.ANY)
    dma = pltpu.SemaphoreType.DMA
    scratch = [
        pltpu.VMEM((16, D), BF),
        pltpu.VMEM((16, 64), F32),
        pltpu.VMEM((2, 8, WIDTH, 128), BF),
        pltpu.VMEM((8, WIDTH, CTX), BF),
        pltpu.VMEM((WIDTH, 256), BF),
        pltpu.VMEM((LAT, 1024), BF),
        pltpu.VMEM((8, 1024, 512), BF),
        pltpu.VMEM((8, 512, FF), BF),
        pltpu.VMEM((FF, D), BF),
        pltpu.VMEM((16, 16, 256), BF),
        pltpu.VMEM((16, 16, WIDTH), BF),
        pltpu.VMEM((15, 16, WIDTH), BF),
        pltpu.VMEM((16, WIDTH), BF),
        pltpu.VMEM((16, LAT), F32),
        pltpu.VMEM((8, 128, LAT), F32),
        pltpu.VMEM((8, 256, 1), F32),
        pltpu.VMEM((8, 256, 1), F32),
        pltpu.VMEM((2, 4, 16, 16, LAT), BF),
        pltpu.VMEM((2, 4, 16, 16, LAT), BF),
        pltpu.VMEM((1024, 128), F32),
        pltpu.VMEM((2, 128, 1024), BF),
        pltpu.VMEM((2, 8, 16, 256), F32),
        pltpu.VMEM((2, 128, FF), F32),
        pltpu.VMEM((2, 128, 1), F32),
        pltpu.VMEM((2, 128, FF), BF),
    ]
    scratch += [
        pltpu.VMEM((16, 8, 128), F32),
        pltpu.VMEM((16, 8, 128), F32),
        pltpu.VMEM((16, 256), BF),
        pltpu.VMEM((16, 16, 256), BF),
        pltpu.VMEM((1024, 128), F32),
        pltpu.VMEM((1024, 128), F32),
    ]
    for gathers in (1, 0):
        for width in (768, 256):
            scratch += [
                pltpu.VMEM((2, 2, 4, 4, 16, width), BF),
                pltpu.VMEM((2, 2, 3, 4, 16, width), BF),
                pltpu.VMEM((2, 2, 4, 16, width), BF),
                pltpu.VMEM((2, 2, 3, 16, width), BF),
            ] + [pltpu.VMEM((2, 2, 4, 4, 16, width), BF)] * gathers
    scratch += [dma((8,)), dma((8,)), dma((7,)), dma((8,))]
    scratch += [dma] * 4 + [dma((2, 2))] * 2 + [dma] * 4 + [dma((12,))] * 2 + [dma((2, 2, 2, 2))] * 2
    scratch += [dma((2, 2, 2))] * 8
    return pl.pallas_call(
        kernel,
        out_shape=jax.ShapeDtypeStruct((2, 8, D), BF),
        in_specs=[pl.BlockSpec(memory_space=pltpu.SMEM)] + [hbm] * 9,
        out_specs=vmem,
        scratch_shapes=scratch,
        compiler_params=pltpu.CompilerParams(
            collective_id=0, has_side_effects=True, vmem_limit_bytes=60 * 1024 * 1024
        ),
    )(lengths, inputs, frequency, queries, cache, down_latent, value_up, output_weight, up_weight, down_weight)


def body(queries, latent_cache, lengths, inputs, down_latent, value_up, output_weight, up_weight, down_weight):
    half = ROPE_BASE ** (-np.arange(32, dtype=np.float32) / np.float32(32))
    frequency = np.tile(half.astype(np.float32), (16, 2))
    return layer(
        lengths, inputs.reshape(16, D), jnp.asarray(frequency),
        jnp.swapaxes(queries, 2, 3), jnp.swapaxes(latent_cache, 1, 2), down_latent.T,
        value_up, output_weight, up_weight.reshape(8, 512, FF), down_weight,
    )


def solution(mesh):
    return jax.shard_map(
        body,
        mesh=mesh,
        in_specs=(
            P(None, ("dp", "tp"), None, None),
            P(("dp", "tp"), None, None),
            P(("dp", "tp")),
            P(None, ("dp", "tp"), None),
            P("tp", None),
            P("tp", None, None),
            P("tp", "dp"),
            P(None, "tp"),
            P("tp", None),
        ),
        out_specs=P(None, ("dp", "tp"), None),
        check_vma=False,
    )
```
